256 devices in a mesh: section: 4 (over x), tensor: 64 (over y, z, core).
Axes of the slice: x: 4, y: 4, z: 8, core: 2. Of those that a mesh axis runs over, the one named last changes fastest.
Arguments:
- inputs: bfloat16 [128, 8192], P(None, 'tensor'), may hold values from -6 to 6
- target: bfloat16 [128, 8192], P(None, 'tensor'), may hold values from -6 to 6
- norm_gains: float32 [4, 8192], P('section'), may hold values from 0.5 to 1.5
- w_query: bfloat16 [4, 64, 512, 2048], P('section', 'tensor'), may hold values from -0.0625 to 0.0625
- w_keyval: bfloat16 [4, 64, 512, 512], P('section', 'tensor'), may hold values from -0.0625 to 0.0625
- w_output: bfloat16 [4, 64, 2048, 512], P('section', 'tensor'), may hold values from -0.0625 to 0.0625
- noise_seed: int32 [1], replicated, may hold values from 0 to 999999
- step_count: int32 [1], replicated, may hold values from 0 to 99999
Outputs:
- layer_outputs: bfloat16 [4, 2, 128, 8192], P('section', None, None, 'tensor')
- losses: float32 [4, 2], P('section')
- new_gains: float32 [4, 8192], P('section')
- new_query: bfloat16 [4, 64, 512, 2048], P('section', 'tensor')
- new_keyval: bfloat16 [4, 64, 512, 512], P('section', 'tensor')
- new_output: bfloat16 [4, 64, 2048, 512], P('section', 'tensor')
The draws below stay inside these ranges and needn't reach their ends.
All inputs are finite; a program needn't handle non-finite values.
Results may differ from the reference program's by a relative error of at most 0.01.
Values may be sent and summed in bfloat16 or wider, within the bound.
No kernel may reach another device: no remote copies, remote signals or barrier semaphores. Data moves between devices by JAX's collectives and lax.ppermute only.
A program may use at most 64 MiB of HBM per device.

```python
import jax
import jax.numpy as jnp
from jax import lax

HEADS = 64
KVH = 8
HD = 128
GROUPS = 4
TOK = 128
D = 8192
SECTIONS = 4
FSPLIT = 16
N_SECTION = 4
N_TENSOR = 64


def level_of(stream_key, shape, shards, low, high):
    def one(dim, parts):
        steps = jax.random.uniform(jax.random.fold_in(jax.random.fold_in(stream_key, 6), dim), (parts,), jnp.float32, low / len(shards), high / len(shards))
        return jnp.repeat(jnp.exp(steps), shape[dim] // parts).reshape((-1,) + (1,) * (len(shape) - dim - 1))

    level = one(*shards[0])
    for cut in shards[1:]:
        level = level * one(*cut)
    return level


def noise(stream_key, shape, spread, most, pieces=(), kind=jnp.bfloat16):
    result = spread * jax.random.normal(stream_key, shape, jnp.float32)
    if pieces:
        result = result * level_of(stream_key, shape, pieces, -0.22, 0.18)
    return jnp.clip(result, -most, most).astype(kind)


def setup_inputs(seed: int = 0) -> dict:
    key_of = jax.random.split(jax.random.key(seed), 9)
    inputs = noise(key_of[0], (TOK, D), 1.0, 6.0, ((1, 64),))
    target = noise(key_of[1], (TOK, D), 1.0, 6.0, ((1, 64),))
    norm_gains = jnp.clip(1.0 + 0.1 * jax.random.normal(key_of[2], (SECTIONS, D), jnp.float32), 0.5, 1.5)
    w_query = noise(key_of[3], (SECTIONS, N_TENSOR, D // FSPLIT, D // GROUPS), D ** -0.5, 0.0625, ((0, 4), (1, 64)))
    w_keyval = noise(key_of[4], (SECTIONS, N_TENSOR, D // FSPLIT, 2 * KVH * HD // GROUPS), D ** -0.5, 0.0625, ((0, 4), (1, 64)))
    w_output = noise(key_of[5], (SECTIONS, N_TENSOR, D // GROUPS, D // FSPLIT), D ** -0.5, 0.0625, ((0, 4), (1, 64)))
    noise_seed = jax.random.randint(key_of[6], (1,), 0, 1000000).astype(jnp.int32)
    step_count = jax.random.randint(key_of[7], (1,), 0, 100000).astype(jnp.int32)
    return dict(inputs=inputs, target=target, norm_gains=norm_gains, w_query=w_query, w_keyval=w_keyval, w_output=w_output, noise_seed=noise_seed, step_count=step_count)


perturb_scale = 0.001
learn_rate = 1e-05
rope_base = 500000.0

def mix_bits(hashed):
    hashed = hashed ^ hashed >> 16 & 65535
    hashed = hashed * 2146121005
    hashed = hashed ^ hashed >> 15 & 131071
    hashed = hashed * -2073254261
    hashed = hashed ^ hashed >> 16 & 65535
    return hashed

def noise_grid(noise_seed, step_count, code, row_ids, col_ids, full_cols):
    salted = mix_bits(mix_bits(step_count[0] * 40503 + code * 1000003) ^ noise_seed[0])
    hashed = mix_bits(mix_bits(row_ids * full_cols + col_ids ^ salted) + salted)
    uniform_part = (hashed >> 8 & 16777215).astype(jnp.float32) * (1.0 / 16777216.0)
    return (uniform_part - 0.5) * 3.4641016

def perturb(weight, noises, amount):
    return (weight.astype(jnp.float32) + amount * noises).astype(jnp.bfloat16)

def rows_to_full(tiles, cols):
    slice_width = D // N_TENSOR
    blocks = tiles.reshape(GROUPS, FSPLIT, GROUPS, slice_width, cols)
    return blocks.transpose(2, 1, 3, 0, 4).reshape(D, GROUPS * cols)

def rows_to_tiles(full, cols):
    slice_width = D // N_TENSOR
    blocks = full.reshape(GROUPS, FSPLIT, slice_width, GROUPS, cols)
    return blocks.transpose(3, 1, 0, 2, 4).reshape(N_TENSOR, GROUPS * slice_width, cols)

def output_to_full(tiles):
    slice_width = D // N_TENSOR
    blocks = tiles.reshape(GROUPS, FSPLIT, D // GROUPS, GROUPS, slice_width)
    return blocks.transpose(0, 2, 3, 1, 4).reshape(D, D)

def output_to_tiles(full):
    slice_width = D // N_TENSOR
    blocks = full.reshape(GROUPS, D // GROUPS, GROUPS, FSPLIT, slice_width)
    return blocks.transpose(0, 3, 1, 2, 4).reshape(N_TENSOR, D // GROUPS, GROUPS * slice_width)

def rotate(values, positions):
    half_width = values.shape[-1] // 2
    frequency = rope_base ** (-jnp.arange(half_width, dtype=jnp.float32) * 2.0 / values.shape[-1])
    angles = positions[:, None] * frequency[None, :]
    cosine = jnp.cos(angles)[:, None, :]
    sine = jnp.sin(angles)[:, None, :]
    first = values[..., :half_width]
    second = values[..., half_width:]
    return jnp.concatenate([first * cosine - second * sine, second * cosine + first * sine], axis=-1)

def attend(queries, keys, values):
    scores = jnp.einsum('qhd,khd->hqk', queries, keys, precision=lax.Precision.HIGHEST) / jnp.sqrt(jnp.float32(queries.shape[-1]))
    row_ids = lax.broadcasted_iota(jnp.int32, scores.shape, 1)
    col_ids = lax.broadcasted_iota(jnp.int32, scores.shape, 2)
    expo = jnp.where(row_ids >= col_ids, jnp.exp(scores), 0.0)
    weights = (expo / lax.optimization_barrier(jnp.sum(expo, axis=-1, keepdims=True))).astype(jnp.bfloat16)
    mixed = jnp.einsum('hqk,khd->qhd', weights.astype(jnp.float32), values.astype(jnp.float32), precision=lax.Precision.HIGHEST)
    return mixed.astype(jnp.bfloat16)

def layer_ref(hidden, gain, query_weight, keyval_weight, output_weight):
    rows_total = hidden.shape[0]
    widened = hidden.astype(jnp.float32)
    squares = lax.optimization_barrier(jnp.sum(widened * widened, axis=1, keepdims=True))
    normed = (widened * lax.rsqrt(squares / D + 1e-05) * gain[None, :]).astype(jnp.bfloat16)
    query = jnp.dot(normed, query_weight, preferred_element_type=jnp.float32)
    keyval = jnp.dot(normed, keyval_weight, preferred_element_type=jnp.float32).astype(jnp.bfloat16)
    positions = jnp.arange(rows_total, dtype=jnp.float32)
    paired = keyval.reshape(rows_total, KVH, 2, HD)
    queries = rotate(query.reshape(rows_total, HEADS, HD), positions)
    keys = rotate(paired[:, :, 0, :].astype(jnp.float32), positions)
    values = paired[:, :, 1, :]
    group_size = HEADS // KVH
    keys = jnp.repeat(keys, group_size, axis=1)
    values = jnp.repeat(values, group_size, axis=1)
    mixed = attend(queries, keys, values).reshape(rows_total, HEADS * HD)
    return (widened + jnp.dot(mixed, output_weight, preferred_element_type=jnp.float32)).astype(jnp.bfloat16)

def section_noise(noise_seed, step_count, section_index):
    kv_width = 2 * KVH * HD
    rows = lax.broadcasted_iota(jnp.int32, (D, 1), 0)
    cols = lax.broadcasted_iota(jnp.int32, (1, D), 1)
    kv_cols = lax.broadcasted_iota(jnp.int32, (1, kv_width), 1)
    first_row = jnp.zeros((1, 1), jnp.int32)
    return (noise_grid(noise_seed, step_count, 4 * section_index, first_row, cols, D)[0], noise_grid(noise_seed, step_count, 4 * section_index + 1, rows, cols, D), noise_grid(noise_seed, step_count, 4 * section_index + 2, rows, kv_cols, kv_width), noise_grid(noise_seed, step_count, 4 * section_index + 3, rows, cols, D))

def reference(inputs, target, norm_gains, w_query, w_keyval, w_output, noise_seed, step_count):
    kv_block = 2 * KVH * HD // GROUPS
    query_block = D // GROUPS
    hidden_pair = [inputs, inputs]
    records = []
    for section_index in range(N_SECTION):
        noises = section_noise(noise_seed, step_count, section_index)
        query_full = rows_to_full(w_query[section_index], query_block)
        keyval_full = rows_to_full(w_keyval[section_index], kv_block)
        output_full = output_to_full(w_output[section_index])
        section_rows = []
        for pass_index, signum in enumerate((1.0, -1.0)):
            amount = signum * perturb_scale
            hidden_pair[pass_index] = layer_ref(hidden_pair[pass_index], norm_gains[section_index] + amount * noises[0], perturb(query_full, noises[1], amount), perturb(keyval_full, noises[2], amount), perturb(output_full, noises[3], amount))
            section_rows.append(hidden_pair[pass_index])
        records.append(jnp.stack(section_rows))
    layer_outputs = jnp.stack(records)
    target_wide = target.astype(jnp.float32)
    plus_gap = hidden_pair[0].astype(jnp.float32) - target_wide
    minus_gap = hidden_pair[1].astype(jnp.float32) - target_wide
    losses = jnp.stack([jnp.sum(plus_gap * plus_gap), jnp.sum(minus_gap * minus_gap)]) / (TOK * D)
    slope = (losses[0] - losses[1]) / (2.0 * perturb_scale)
    step_size = learn_rate * slope
    gain_list, query_list, keyval_list, output_list = ([], [], [], [])
    for section_index in range(N_SECTION):
        noises = section_noise(noise_seed, step_count, section_index)
        query_full = rows_to_full(w_query[section_index], query_block)
        keyval_full = rows_to_full(w_keyval[section_index], kv_block)
        output_full = output_to_full(w_output[section_index])
        gain_list.append(norm_gains[section_index] - step_size * noises[0])
        query_list.append(rows_to_tiles((query_full.astype(jnp.float32) - step_size * noises[1]).astype(jnp.bfloat16), query_block))
        keyval_list.append(rows_to_tiles((keyval_full.astype(jnp.float32) - step_size * noises[2]).astype(jnp.bfloat16), kv_block))
        output_list.append(output_to_tiles((output_full.astype(jnp.float32) - step_size * noises[3]).astype(jnp.bfloat16)))
    section_losses = jnp.broadcast_to(losses[None, :], (N_SECTION, 2))
    return (layer_outputs, section_losses, jnp.stack(gain_list), jnp.stack(query_list), jnp.stack(keyval_list), jnp.stack(output_list))
```

```python
import functools

import jax
import jax.numpy as jnp
import numpy as np
from jax import lax
from jax.experimental import pallas as pl
from jax.experimental.pallas import tpu as pltpu
from jax.sharding import Mesh, PartitionSpec as P

HD = 128
NY, NZ, NC = 4, 8, 2
LANE = 128

perturb_scale = 0.001
learn_rate = 1e-05
rope_base = 500000.0


def logical(value, by):
    return lax.shift_right_logical(value, jnp.full(value.shape, by, value.dtype))


def mix_bits(hashed):
    hashed = hashed ^ logical(hashed, 16)
    hashed = hashed * jnp.int32(2146121005)
    hashed = hashed ^ logical(hashed, 15)
    hashed = hashed * jnp.int32(-2073254261)
    hashed = hashed ^ logical(hashed, 16)
    return hashed


def noise_of(index, salt):
    hashed = mix_bits(mix_bits(index ^ salt) + salt)
    uniform_part = logical(hashed, 8).astype(jnp.float32) * (1.0 / 16777216.0)
    return (uniform_part - 0.5) * 3.4641016


def perturb_kernel(row_step, row_jump, col_jump, rows, ints_ref, sign_ref, w_ref, z_ref, mine_ref, other_ref):
    step = pl.program_id(0)
    shape = w_ref.shape
    row = lax.broadcasted_iota(jnp.int32, (shape[0], 1), 0) + step * rows
    col = lax.broadcasted_iota(jnp.int32, (1, shape[1]), 1)
    row_part = row * row_step + logical(row, 7) * row_jump + ints_ref[1]
    col_part = col + logical(col, 7) * col_jump
    z = noise_of(row_part + col_part, ints_ref[0])
    z_ref[...] = z
    w = w_ref[...].astype(jnp.float32)
    shift = sign_ref[0] * z
    mine_ref[...] = (w + shift).astype(jnp.bfloat16)
    other_ref[...] = (w - shift).astype(jnp.bfloat16)


def perturbed(w, salt, base, amount, row_step, row_jump, col_jump, steps):
    rows = w.shape[0] // steps
    spec = pl.BlockSpec((rows, w.shape[1]), lambda i: (i, 0))


    return pl.pallas_call(
        functools.partial(perturb_kernel, row_step, row_jump, col_jump, rows),
        grid=(steps,),
        in_specs=[
            pl.BlockSpec(memory_space=pltpu.SMEM),
            pl.BlockSpec(memory_space=pltpu.SMEM),
            spec,
        ],
        out_specs=[spec, spec, spec],
        out_shape=[
            jax.ShapeDtypeStruct(w.shape, jnp.float32),
            jax.ShapeDtypeStruct(w.shape, jnp.bfloat16),
            jax.ShapeDtypeStruct(w.shape, jnp.bfloat16),
        ],
        compiler_params=pltpu.CompilerParams(vmem_limit_bytes=32 * 1024 * 1024),
    )(jnp.stack([salt, base]), amount.reshape(1), w)


def shifted(array, axis, count, by):
    return lax.ppermute(array, axis, [(i, (i + by) % count) for i in range(count)])


def swapped(array):
    return lax.ppermute(array, "core", [(0, 1), (1, 0)])


def rope_tables(tokens):
    half = HD // 2
    frequency = np.float32(rope_base) ** (-np.arange(half, dtype=np.float32) * np.float32(2.0) / np.float32(HD))
    angles = np.arange(tokens, dtype=np.float32)[:, None] * frequency.astype(np.float32)[None, :]
    cosine = np.cos(angles.astype(np.float64)).astype(np.float32)
    sine = np.sin(angles.astype(np.float64)).astype(np.float32)
    return np.concatenate([cosine, cosine], 1), np.concatenate([-sine, sine], 1)


def rotate(values, cosine, sine):
    half = HD // 2
    turned = jnp.concatenate([values[:, half:], values[:, :half]], axis=1)
    return values * cosine + turned * sine


def local(inputs, target, norm_gains, w_query, w_keyval, w_output, noise_seed, step_count):
    section = lax.axis_index("section")
    sections = lax.axis_size("section")
    y = lax.axis_index("y")
    z = lax.axis_index("z")
    core = lax.axis_index("core")
    tokens, width = inputs.shape
    full = width * NY * NZ * NC
    query_cols = w_query.shape[3]
    keyval_cols = w_keyval.shape[3]
    block = z * NC + core
    amount = jnp.where(core == 0, perturb_scale, -perturb_scale).astype(jnp.float32)

    def salt(code):
        return mix_bits(mix_bits(step_count[0] * 40503 + (4 * section + code) * 1000003) ^ noise_seed[0])

    spread = NZ * NC * width
    zq, q_mine, q_other = perturbed(
        w_query[0, 0], salt(1), block * width * full + y * query_cols, amount,
        full, (spread - width) * full, 0, 4,
    )
    zk, k_mine, k_other = perturbed(
        w_keyval[0, 0], salt(2), block * width * keyval_cols * NY + y * keyval_cols, amount,
        keyval_cols * NY, (spread - width) * keyval_cols * NY, 0, 2,
    )
    q_part = swapped(q_other)
    k_part = swapped(k_other)
    zo, o_mine, o_other = perturbed(
        w_output[0, 0], salt(3), y * query_cols * full + block * width, amount,
        full, 0, spread - width, 4,
    )
    o_part = swapped(o_other)

    gain_noise = noise_of(jnp.arange(full, dtype=jnp.int32), salt(0))
    gains = (norm_gains[0] + amount * gain_noise).reshape(NY, NZ, NC, width)
    gains = lax.dynamic_index_in_dim(gains, z, 1, keepdims=False)
    gains = jnp.where(core == 0, gains, gains[:, ::-1])
    gains = gains.transpose(1, 0, 2).reshape(NC, 1, NY * width)

    cosine, sine = (jnp.asarray(t) for t in rope_tables(tokens))
    causal = lax.broadcasted_iota(jnp.int32, (tokens, tokens), 0) >= lax.broadcasted_iota(
        jnp.int32, (tokens, tokens), 1
    )

    hidden = jnp.stack([inputs, swapped(inputs)])
    goal = jnp.stack([target, swapped(target)])
    record = jnp.zeros_like(hidden)
    for tick in range(4):
        around = jnp.stack([hidden] + [shifted(hidden, "y", NY, k) for k in range(1, NY)])
        blocks = jnp.stack(
            [lax.dynamic_index_in_dim(around, (y - j) % NY, 0, keepdims=False) for j in range(NY)]
        )
        wide = blocks.transpose(1, 2, 0, 3).reshape(NC, tokens, NY * width).astype(jnp.float32)
        squares = jnp.sum(wide * wide, axis=(0, 2))
        scaled = (wide * gains).astype(jnp.bfloat16)
        query = jnp.dot(scaled[0], q_mine, preferred_element_type=jnp.float32) + jnp.dot(
            scaled[1], q_part, preferred_element_type=jnp.float32
        )
        keyval = jnp.dot(scaled[0], k_mine, preferred_element_type=jnp.float32) + jnp.dot(
            scaled[1], k_part, preferred_element_type=jnp.float32
        )
        heads_z = query_cols // HD // NZ
        query = query.astype(jnp.bfloat16).reshape(tokens, NZ, heads_z, HD).transpose(1, 2, 0, 3)
        keyval = keyval.astype(jnp.bfloat16).reshape(tokens, 2, 2, HD).transpose(1, 2, 0, 3)
        keyval = jnp.repeat(keyval, NZ // 2, axis=0)
        high = squares.astype(jnp.bfloat16)
        low = (squares - high.astype(jnp.float32)).astype(jnp.bfloat16)
        extra = jnp.concatenate([high[None], low[None], jnp.zeros((14, tokens), jnp.bfloat16)])
        extra = jnp.broadcast_to(extra[None], (NZ, 16, tokens))
        payload = jnp.concatenate(
            [query.reshape(NZ, -1, HD), keyval.reshape(NZ, -1, HD), extra], axis=1
        )
        received = lax.all_to_all(payload, "z", 0, 0, tiled=True)
        summed = jnp.sum(received.astype(jnp.float32), axis=0)
        queries = summed[: heads_z * tokens].reshape(heads_z, tokens, HD)
        key = summed[heads_z * tokens : (heads_z + 1) * tokens]
        value = summed[(heads_z + 1) * tokens : (heads_z + 2) * tokens]
        total = summed[(heads_z + 2) * tokens] + summed[(heads_z + 2) * tokens + 1]
        inverse = lax.rsqrt(total / full + 1e-05)[:, None]
        key = rotate((key * inverse).astype(jnp.bfloat16).astype(jnp.float32), cosine, sine)
        value = (value * inverse).astype(jnp.bfloat16)
        mixed = []
        for head in range(heads_z):
            rotated = rotate(queries[head] * inverse, cosine, sine)
            scores = lax.dot_general(
                rotated, key, (((1,), (1,)), ((), ())), precision=lax.Precision.HIGHEST
            ) / jnp.sqrt(jnp.float32(HD))
            expo = jnp.where(causal, jnp.exp(scores), 0.0)
            weights = (expo / jnp.sum(expo, axis=-1, keepdims=True)).astype(jnp.bfloat16)
            mixed.append(
                jnp.dot(weights, value, preferred_element_type=jnp.float32).astype(jnp.bfloat16)
            )
        mixed = jnp.stack(mixed)
        mixed = jnp.broadcast_to(mixed[None], (NZ,) + mixed.shape)
        heads = lax.all_to_all(mixed, "z", 0, 0, tiled=True)
        heads = heads.transpose(2, 0, 1, 3).reshape(tokens, query_cols)
        projected = jnp.stack(
            [
                jnp.dot(heads, o_mine, preferred_element_type=jnp.float32),
                jnp.dot(heads, o_part, preferred_element_type=jnp.float32),
            ]
        ).reshape(NC, tokens, NY, width).transpose(2, 0, 1, 3)
        result = hidden.astype(jnp.float32) + lax.dynamic_index_in_dim(projected, y, 0, keepdims=False)
        for k in range(1, NY):
            piece = lax.dynamic_index_in_dim(projected, (y + k) % NY, 0, keepdims=False)
            result = result + shifted(piece.astype(jnp.bfloat16), "y", NY, k).astype(jnp.float32)
        result = result.astype(jnp.bfloat16)
        record = jnp.where(section == tick, result, record)
        if tick < 3:
            hidden = lax.ppermute(result, "section", [(tick, tick + 1)])

    gap = result.astype(jnp.float32) - goal.astype(jnp.float32)
    squared = jnp.sum(gap * gap)
    squared = jnp.where((jnp.arange(2) == core) & (section == sections - 1), squared, 0.0)
    squared = lax.psum(squared, "core")
    squared = lax.psum(squared, "y")
    squared = lax.psum(squared, "z")
    squared = lax.psum(squared, "section")
    losses = squared / (tokens * full)
    rate = learn_rate * ((losses[0] - losses[1]) / (2.0 * perturb_scale))
    new_gains = (norm_gains[0] - rate * gain_noise)[None]

    def updated(w, noise):
        return (w[0, 0].astype(jnp.float32) - rate * noise).astype(jnp.bfloat16)[None, None]

    mine, other = record[0], swapped(record[1])
    layer_outputs = jnp.where(core == 0, jnp.stack([mine, other]), jnp.stack([other, mine]))[None]
    return (
        layer_outputs,
        losses[None],
        new_gains,
        updated(w_query, zq),
        updated(w_keyval, zk),
        updated(w_output, zo),
    )


def solution(mesh):
    mesh = Mesh(mesh.devices.reshape(-1, NY, NZ, NC), ("section", "y", "z", "core"))
    tensor = ("y", "z", "core")
    return jax.shard_map(
        local,
        mesh=mesh,
        in_specs=(
            P(None, tensor),
            P(None, tensor),
            P("section", None),
            P("section", tensor, None, None),
            P("section", tensor, None, None),
            P("section", tensor, None, None),
            P(),
            P(),
        ),
        out_specs=(
            P("section", None, None, tensor),
            P("section", None),
            P("section", None),
            P("section", tensor, None, None),
            P("section", tensor, None, None),
            P("section", tensor, None, None),
        ),
        check_vma=False,
    )
```

```python
import functools

import jax
import jax.numpy as jnp
import numpy as np
from jax import lax
from jax.experimental import pallas as pl
from jax.experimental.pallas import tpu as pltpu
from jax.sharding import Mesh, PartitionSpec as P

HD = 128
NY, NZ, NC = 4, 8, 2
LANE = 128

perturb_scale = 0.001
learn_rate = 1e-05
rope_base = 500000.0


def logical(value, by):
    return lax.shift_right_logical(value, jnp.full(value.shape, by, value.dtype))


def mix_bits(hashed):
    hashed = hashed ^ logical(hashed, 16)
    hashed = hashed * jnp.int32(2146121005)
    hashed = hashed ^ logical(hashed, 15)
    hashed = hashed * jnp.int32(-2073254261)
    hashed = hashed ^ logical(hashed, 16)
    return hashed


def noise_of(index, salt):
    hashed = mix_bits(mix_bits(index ^ salt) + salt)
    uniform_part = logical(hashed, 8).astype(jnp.float32) * (1.0 / 16777216.0)
    return (uniform_part - 0.5) * 3.4641016


def perturb_kernel(row_step, row_jump, col_jump, rows, ints_ref, sign_ref, w_ref, z_ref, mine_ref, other_ref):
    step = pl.program_id(0)
    shape = w_ref.shape
    row = lax.broadcasted_iota(jnp.int32, (shape[0], 1), 0) + step * rows
    col = lax.broadcasted_iota(jnp.int32, (1, shape[1]), 1)
    row_part = row * row_step + logical(row, 7) * row_jump + ints_ref[1]
    col_part = col + logical(col, 7) * col_jump
    z = noise_of(row_part + col_part, ints_ref[0])
    z_ref[...] = z
    w = w_ref[...].astype(jnp.float32)
    shift = sign_ref[0] * z
    mine_ref[...] = (w + shift).astype(jnp.bfloat16)
    other_ref[...] = (w - shift).astype(jnp.bfloat16)


def perturbed(w, salt, base, amount, row_step, row_jump, col_jump, steps):
    rows = w.shape[0] // steps
    spec = pl.BlockSpec((rows, w.shape[1]), lambda i: (i, 0))


    return pl.pallas_call(
        functools.partial(perturb_kernel, row_step, row_jump, col_jump, rows),
        grid=(steps,),
        in_specs=[
            pl.BlockSpec(memory_space=pltpu.SMEM),
            pl.BlockSpec(memory_space=pltpu.SMEM),
            spec,
        ],
        out_specs=[spec, spec, spec],
        out_shape=[
            jax.ShapeDtypeStruct(w.shape, jnp.float32),
            jax.ShapeDtypeStruct(w.shape, jnp.bfloat16),
            jax.ShapeDtypeStruct(w.shape, jnp.bfloat16),
        ],
        compiler_params=pltpu.CompilerParams(vmem_limit_bytes=32 * 1024 * 1024),
    )(jnp.stack([salt, base]), amount.reshape(1), w)


def shifted(array, axis, count, by):
    return lax.ppermute(array, axis, [(i, (i + by) % count) for i in range(count)])


def swapped(array):
    return lax.ppermute(array, "core", [(0, 1), (1, 0)])


def rope_tables(tokens):
    half = HD // 2
    frequency = np.float32(rope_base) ** (-np.arange(half, dtype=np.float32) * np.float32(2.0) / np.float32(HD))
    angles = np.arange(tokens, dtype=np.float32)[:, None] * frequency.astype(np.float32)[None, :]
    cosine = np.cos(angles.astype(np.float64)).astype(np.float32)
    sine = np.sin(angles.astype(np.float64)).astype(np.float32)
    return np.concatenate([cosine, cosine], 1), np.concatenate([-sine, sine], 1)


def rotate(values, cosine, sine):
    return values * cosine + pltpu.roll(values, HD // 2, 1) * sine


def same_index(size):
    return lax.broadcasted_iota(jnp.int32, (size, size), 0) == lax.broadcasted_iota(
        jnp.int32, (size, size), 1
    )


def project_kernel(y_ref, *refs):
    around = refs[:NY]
    gains_ref, q_mine, q_part, k_mine, k_part, out_ref, scaled = refs[NY:]
    tokens, width = around[0].shape[1:]
    total = jnp.zeros((tokens, 1), jnp.float32)
    for k in range(NY):
        place = pl.multiple_of(lax.rem(y_ref[0] + (NY - k), NY) * width, width)
        for half in range(NC):
            wide = around[k][half].astype(jnp.float32)
            total = total + jnp.sum(wide * wide, axis=1, keepdims=True)
            scaled[half, :, pl.ds(place, width)] = (wide * gains_ref[half, k : k + 1, :]).astype(jnp.bfloat16)

    def product(mine, part, start, size):
        return jnp.dot(
            scaled[0], mine[:, start : start + size], preferred_element_type=jnp.float32
        ) + jnp.dot(scaled[1], part[:, start : start + size], preferred_element_type=jnp.float32)

    span = q_mine.shape[1] // NZ
    kept = span // HD * tokens
    groups = k_mine.shape[1] // (2 * HD)
    for dest in range(NZ):
        query = product(q_mine, q_part, dest * span, span).astype(jnp.bfloat16)
        for head in range(span // HD):
            out_ref[dest, head * tokens : (head + 1) * tokens, :] = query[:, head * HD : (head + 1) * HD]
    for group in range(groups):
        keyval = product(k_mine, k_part, group * 2 * HD, 2 * HD).astype(jnp.bfloat16)
        for dest in range(group * NZ // groups, (group + 1) * NZ // groups):
            out_ref[dest, kept : kept + tokens, :] = keyval[:, :HD]
            out_ref[dest, kept + tokens : kept + 2 * tokens, :] = keyval[:, HD:]
    row = jnp.sum(jnp.where(same_index(tokens), total, 0.0), axis=0, keepdims=True)
    high = row.astype(jnp.bfloat16).astype(jnp.float32)
    line = lax.broadcasted_iota(jnp.int32, (16, tokens), 0)
    extra = jnp.where(line == 0, high, jnp.where(line == 1, row - high, 0.0)).astype(jnp.bfloat16)
    for dest in range(NZ):
        out_ref[dest, kept + 2 * tokens :, :] = extra


def attend_kernel(full, recv_ref, cos_ref, sin_ref, out_ref):
    tokens = cos_ref.shape[0]
    heads = out_ref.shape[1] // tokens

    def total(start, size):
        acc = recv_ref[0, start : start + size, :].astype(jnp.float32)
        for source in range(1, NZ):
            acc = acc + recv_ref[source, start : start + size, :].astype(jnp.float32)
        return acc

    cosine = cos_ref[...]
    sine = sin_ref[...]
    kept = heads * tokens
    squares = total(kept + 2 * tokens, 16)
    row = squares[0:1] + squares[1:2]
    column = jnp.sum(jnp.where(same_index(tokens), row, 0.0), axis=1, keepdims=True)
    inverse = lax.rsqrt(column / full + 1e-05)
    key = (total(kept, tokens) * inverse).astype(jnp.bfloat16).astype(jnp.float32)
    key = rotate(key, cosine, sine)
    value = (total(kept + tokens, tokens) * inverse).astype(jnp.bfloat16)
    causal = lax.broadcasted_iota(jnp.int32, (tokens, tokens), 0) >= lax.broadcasted_iota(
        jnp.int32, (tokens, tokens), 1
    )
    for head in range(heads):
        query = rotate(total(head * tokens, tokens) * inverse, cosine, sine)
        scores = lax.dot_general(
            query, key, (((1,), (1,)), ((), ())),
            precision=lax.Precision.HIGHEST, preferred_element_type=jnp.float32,
        ) * (1.0 / np.sqrt(np.float32(HD)))
        expo = jnp.where(causal, jnp.exp(scores), 0.0)
        weights = (expo / jnp.sum(expo, axis=1, keepdims=True)).astype(jnp.bfloat16)
        mixed = jnp.dot(weights, value, preferred_element_type=jnp.float32).astype(jnp.bfloat16)
        for dest in range(NZ):
            out_ref[dest, head * tokens : (head + 1) * tokens, :] = mixed


def output_kernel(y_ref, heads_ref, o_mine, o_part, hidden_ref, base_ref, *refs):
    sent = refs[: NY - 1]
    joined, pieces = refs[NY - 1 :]
    tokens, width = hidden_ref.shape[1:]
    for source in range(heads_ref.shape[0]):
        for head in range(heads_ref.shape[1] // tokens):
            at = (source * (heads_ref.shape[1] // tokens) + head) * HD
            joined[:, at : at + HD] = heads_ref[source, head * tokens : (head + 1) * tokens, :]
    for half, weight in enumerate((o_mine, o_part)):
        for pair in range(NY // 2):
            at = pair * 2 * width
            product = jnp.dot(
                joined[...], weight[:, at : at + 2 * width], preferred_element_type=jnp.float32
            )
            for inner in range(2):
                step = lax.rem(pair * 2 + inner + NY - y_ref[0], NY)
                pieces[step, half] = product[:, inner * width : (inner + 1) * width]
    base_ref[...] = hidden_ref[...].astype(jnp.float32) + pieces[0]
    for k in range(1, NY):
        sent[k - 1][...] = pieces[k].astype(jnp.bfloat16)


VMEM = pl.BlockSpec(memory_space=pltpu.VMEM)
SMEM = pl.BlockSpec(memory_space=pltpu.SMEM)
PARAMS = pltpu.CompilerParams(vmem_limit_bytes=40 * 1024 * 1024)


def summed_over(value, axis, steps):
    count = lax.axis_size(axis)
    got = [
        lax.ppermute(value, axis, [(i, i ^ step) for i in range(count)]) for step in steps
    ]
    if len(got) == 1:
        return value + got[0]
    return (value + got[0]) + (got[1] + got[2])


def local(inputs, target, norm_gains, w_query, w_keyval, w_output, noise_seed, step_count):
    section = lax.axis_index("section")
    sections = lax.axis_size("section")
    y = lax.axis_index("y")
    z = lax.axis_index("z")
    core = lax.axis_index("core")
    tokens, width = inputs.shape
    full = width * NY * NZ * NC
    query_cols = w_query.shape[3]
    keyval_cols = w_keyval.shape[3]
    block = z * NC + core
    amount = jnp.where(core == 0, perturb_scale, -perturb_scale).astype(jnp.float32)

    def salt(code):
        return mix_bits(mix_bits(step_count[0] * 40503 + (4 * section + code) * 1000003) ^ noise_seed[0])

    spread = NZ * NC * width
    zq, q_mine, q_other = perturbed(
        w_query[0, 0], salt(1), block * width * full + y * query_cols, amount,
        full, (spread - width) * full, 0, 4,
    )
    zk, k_mine, k_other = perturbed(
        w_keyval[0, 0], salt(2), block * width * keyval_cols * NY + y * keyval_cols, amount,
        keyval_cols * NY, (spread - width) * keyval_cols * NY, 0, 2,
    )
    q_part = swapped(q_other)
    k_part = swapped(k_other)
    zo, o_mine, o_other = perturbed(
        w_output[0, 0], salt(3), y * query_cols * full + block * width, amount,
        full, 0, spread - width, 4,
    )
    o_part = swapped(o_other)

    gain_noise = noise_of(jnp.arange(full, dtype=jnp.int32), salt(0))
    gains = (norm_gains[0] + amount * gain_noise).reshape(NY, NZ, NC, width)
    gains = lax.dynamic_index_in_dim(gains, z, 1, keepdims=False)
    gains = jnp.where(core == 0, gains, gains[:, ::-1])
    gains = jnp.take(gains.transpose(1, 0, 2), (y - jnp.arange(NY)) % NY, axis=1)

    cosine, sine = (jnp.asarray(t) for t in rope_tables(tokens))
    place = y.reshape(1)
    heads_z = query_cols // HD // NZ
    rows = (heads_z + 2) * tokens + 16

    def project(around):
        return pl.pallas_call(
            project_kernel,
            in_specs=[SMEM] + [VMEM] * (NY + 5),
            out_specs=VMEM,
            out_shape=jax.ShapeDtypeStruct((NZ, rows, HD), jnp.bfloat16),
            scratch_shapes=[pltpu.VMEM((NC, tokens, NY * width), jnp.bfloat16)],
            compiler_params=PARAMS,
        )(place, *around, gains, q_mine, q_part, k_mine, k_part)

    def attend(received):
        return pl.pallas_call(
            functools.partial(attend_kernel, full),
            in_specs=[VMEM] * 3,
            out_specs=VMEM,
            out_shape=jax.ShapeDtypeStruct((NZ, heads_z * tokens, HD), jnp.bfloat16),
            compiler_params=PARAMS,
        )(received, cosine, sine)

    def output(heads, hidden):
        return pl.pallas_call(
            output_kernel,
            in_specs=[SMEM] + [VMEM] * 4,
            out_specs=[VMEM] * NY,
            out_shape=[jax.ShapeDtypeStruct(hidden.shape, jnp.float32)]
            + [jax.ShapeDtypeStruct(hidden.shape, jnp.bfloat16)] * (NY - 1),
            scratch_shapes=[
                pltpu.VMEM((tokens, query_cols), jnp.bfloat16),
                pltpu.VMEM((NY,) + hidden.shape, jnp.float32),
            ],
            compiler_params=PARAMS,
        )(place, heads, o_mine, o_part, hidden)

    hidden = jnp.stack([inputs, swapped(inputs)])
    goal = jnp.stack([target, swapped(target)])
    record = jnp.zeros_like(hidden)
    for tick in range(4):
        around = [hidden] + [shifted(hidden, "y", NY, k) for k in range(1, NY)]
        received = lax.all_to_all(project(around), "z", 0, 0, tiled=True)
        heads = lax.all_to_all(attend(received), "z", 0, 0, tiled=True)
        base, *pieces = output(heads, hidden)
        for k in range(1, NY):
            base = base + shifted(pieces[k - 1], "y", NY, k).astype(jnp.float32)
        result = base.astype(jnp.bfloat16)
        record = jnp.where(section == tick, result, record)
        if tick < 3:
            hidden = lax.ppermute(result, "section", [(tick, tick + 1)])

    gap = result.astype(jnp.float32) - goal.astype(jnp.float32)
    squared = jnp.sum(gap * gap)
    squared = jnp.full((8, LANE), squared)
    squared = summed_over(squared, "y", (1, 2, 3))
    squared = summed_over(squared, "z", (1,))
    squared = summed_over(squared, "z", (2, 4, 6))
    copies = [lax.ppermute(squared, "section", [(sections - 1, k)]) for k in range(sections - 1)]
    squared = jnp.where(section == sections - 1, squared, sum(copies[1:], copies[0]))
    partner = swapped(squared)
    squared = jnp.where(core == 0, jnp.stack([squared, partner]), jnp.stack([partner, squared]))[:, 0, 0]
    losses = squared / (tokens * full)
    rate = learn_rate * ((losses[0] - losses[1]) / (2.0 * perturb_scale))
    new_gains = (norm_gains[0] - rate * gain_noise)[None]

    def updated(w, noise):
        return (w[0, 0].astype(jnp.float32) - rate * noise).astype(jnp.bfloat16)[None, None]

    mine, other = record[0], swapped(record[1])
    layer_outputs = jnp.where(core == 0, jnp.stack([mine, other]), jnp.stack([other, mine]))[None]
    return (
        layer_outputs,
        losses[None],
        new_gains,
        updated(w_query, zq),
        updated(w_keyval, zk),
        updated(w_output, zo),
    )


def solution(mesh):
    mesh = Mesh(mesh.devices.reshape(-1, NY, NZ, NC), ("section", "y", "z", "core"))
    tensor = ("y", "z", "core")
    return jax.shard_map(
        local,
        mesh=mesh,
        in_specs=(
            P(None, tensor),
            P(None, tensor),
            P("section", None),
            P("section", tensor, None, None),
            P("section", tensor, None, None),
            P("section", tensor, None, None),
            P(),
            P(),
        ),
        out_specs=(
            P("section", None, None, tensor),
            P("section", None),
            P("section", None),
            P("section", tensor, None, None),
            P("section", tensor, None, None),
            P("section", tensor, None, None),
        ),
        check_vma=False,
    )
```

```python
import functools

import jax
import jax.numpy as jnp
import numpy as np
from jax import lax
from jax.experimental import pallas as pl
from jax.experimental.pallas import tpu as pltpu
from jax.sharding import Mesh, PartitionSpec as P

HD = 128
NY, NZ, NC = 4, 8, 2
LANE = 128

perturb_scale = 0.001
learn_rate = 1e-05
rope_base = 500000.0


def logical(value, by):
    return lax.shift_right_logical(value, jnp.full(value.shape, by, value.dtype))


def mix_bits(hashed):
    hashed = hashed ^ logical(hashed, 16)
    hashed = hashed * jnp.int32(2146121005)
    hashed = hashed ^ logical(hashed, 15)
    hashed = hashed * jnp.int32(-2073254261)
    hashed = hashed ^ logical(hashed, 16)
    return hashed


def noise_of(index, salt):
    hashed = mix_bits(mix_bits(index ^ salt) + salt)
    uniform_part = logical(hashed, 8).astype(jnp.float32) * (1.0 / 16777216.0)
    return (uniform_part - 0.5) * 3.4641016


def limit(mib):
    return pltpu.CompilerParams(vmem_limit_bytes=mib * 1024 * 1024)


def perturb_input_kernel(full, spread, groups, ints_ref, sign_ref, q_ref, k_ref, zq_ref, zk_ref, mine_ref, other_ref):
    rows, query_cols = q_ref.shape
    keyval_cols = k_ref.shape[1]
    row = lax.broadcasted_iota(jnp.int32, (rows, 1), 0) + pl.program_id(0) * spread + ints_ref[2]
    for w_ref, z_ref, at, salt, cols, first in (
        (q_ref, zq_ref, 0, ints_ref[0], full, ints_ref[3]),
        (k_ref, zk_ref, query_cols, ints_ref[1], keyval_cols * groups, ints_ref[4]),
    ):
        width = w_ref.shape[1]
        col = lax.broadcasted_iota(jnp.int32, (1, width), 1) + first
        z = noise_of(row * cols + col, salt)
        z_ref[...] = z
        w = w_ref[...].astype(jnp.float32)
        shift = sign_ref[0] * z
        mine_ref[:, at : at + width] = (w + shift).astype(jnp.bfloat16)
        other_ref[:, at : at + width] = (w - shift).astype(jnp.bfloat16)


def perturb_output_kernel(full, spread, width, ints_ref, sign_ref, w_ref, z_ref, mine_ref, other_ref):
    rows, cols = w_ref.shape
    row = lax.broadcasted_iota(jnp.int32, (rows, 1), 0) + pl.program_id(0) * rows + ints_ref[1]
    col = lax.broadcasted_iota(jnp.int32, (1, cols), 1)
    col = col + col // width * (spread - width) + ints_ref[2]
    z = noise_of(row * full + col, ints_ref[0])
    z_ref[...] = z
    w = w_ref[...].astype(jnp.float32)
    shift = sign_ref[0] * z
    mine_ref[...] = (w + shift).astype(jnp.bfloat16)
    other_ref[...] = (w - shift).astype(jnp.bfloat16)


def update_kernel(rate_ref, *refs):
    count = len(refs) // 3
    for w_ref, z_ref, out_ref in zip(refs[:count], refs[count : 2 * count], refs[2 * count :]):
        out_ref[...] = (w_ref[...].astype(jnp.float32) - rate_ref[0] * z_ref[...]).astype(jnp.bfloat16)


def by_rows(array, steps):
    return pl.BlockSpec((array.shape[0] // steps, array.shape[1]), lambda i: (i, 0))


def noise_cost(count):
    return pl.CostEstimate(flops=60 * count, bytes_accessed=10 * count, transcendentals=0)


def shifted(array, axis, count, by):
    return lax.ppermute(array, axis, [(i, (i + by) % count) for i in range(count)])


def swapped(array):
    return lax.ppermute(array, "core", [(0, 1), (1, 0)])


def rope_tables(tokens):
    half = HD // 2
    frequency = np.float32(rope_base) ** (-np.arange(half, dtype=np.float32) * np.float32(2.0) / np.float32(HD))
    angles = np.arange(tokens, dtype=np.float32)[:, None] * frequency.astype(np.float32)[None, :]
    cosine = np.cos(angles.astype(np.float64)).astype(np.float32)
    sine = np.sin(angles.astype(np.float64)).astype(np.float32)
    return np.concatenate([cosine, cosine], 1), np.concatenate([-sine, sine], 1)


def rotate(values, cosine, sine):
    return values * cosine + pltpu.roll(values, HD // 2, 1) * sine


def same_index(size):
    return lax.broadcasted_iota(jnp.int32, (size, size), 0) == lax.broadcasted_iota(
        jnp.int32, (size, size), 1
    )


def project_kernel(y_ref, *refs):
    around = refs[:NY]
    gains_ref, mine, part, out_ref, scaled = refs[NY:]
    tokens, width = around[0].shape[1:]
    total = jnp.zeros((tokens, 1), jnp.float32)
    for k in range(NY):
        place = pl.multiple_of(lax.rem(y_ref[0] + (NY - k), NY) * width, width)
        for half in range(NC):
            wide = around[k][half].astype(jnp.float32)
            total = total + jnp.sum(wide * wide, axis=1, keepdims=True)
            scaled[half, :, pl.ds(place, width)] = (wide * gains_ref[half, k : k + 1, :]).astype(jnp.bfloat16)

    def product(start, size):
        return jnp.dot(
            scaled[0], mine[:, start : start + size], preferred_element_type=jnp.float32
        ) + jnp.dot(scaled[1], part[:, start : start + size], preferred_element_type=jnp.float32)

    kept = out_ref.shape[1] - 16 - 2 * tokens
    span = kept // tokens * HD
    for dest in range(NZ):
        query = product(dest * span, span).astype(jnp.bfloat16)
        for head in range(span // HD):
            out_ref[dest, head * tokens : (head + 1) * tokens, :] = query[:, head * HD : (head + 1) * HD]
    groups = (mine.shape[1] - NZ * span) // (2 * HD)
    for group in range(groups):
        keyval = product(NZ * span + group * 2 * HD, 2 * HD).astype(jnp.bfloat16)
        for dest in range(group * NZ // groups, (group + 1) * NZ // groups):
            out_ref[dest, kept : kept + tokens, :] = keyval[:, :HD]
            out_ref[dest, kept + tokens : kept + 2 * tokens, :] = keyval[:, HD:]
    row = jnp.sum(jnp.where(same_index(tokens), total, 0.0), axis=0, keepdims=True)
    high = row.astype(jnp.bfloat16).astype(jnp.float32)
    line = lax.broadcasted_iota(jnp.int32, (16, tokens), 0)
    extra = jnp.where(line == 0, high, jnp.where(line == 1, row - high, 0.0)).astype(jnp.bfloat16)
    for dest in range(NZ):
        out_ref[dest, kept + 2 * tokens :, :] = extra


def attend_kernel(full, recv_ref, cos_ref, sin_ref, out_ref):
    tokens = cos_ref.shape[0]
    heads = out_ref.shape[1] // tokens

    def total(start, size):
        acc = recv_ref[0, start : start + size, :].astype(jnp.float32)
        for source in range(1, NZ):
            acc = acc + recv_ref[source, start : start + size, :].astype(jnp.float32)
        return acc

    cosine = cos_ref[...]
    sine = sin_ref[...]
    kept = heads * tokens
    squares = total(kept + 2 * tokens, 16)
    row = squares[0:1] + squares[1:2]
    column = jnp.sum(jnp.where(same_index(tokens), row, 0.0), axis=1, keepdims=True)
    inverse = lax.rsqrt(column / full + 1e-05)
    key = (total(kept, tokens) * inverse).astype(jnp.bfloat16).astype(jnp.float32)
    key = rotate(key, cosine, sine)
    value = (total(kept + tokens, tokens) * inverse).astype(jnp.bfloat16)
    causal = lax.broadcasted_iota(jnp.int32, (tokens, tokens), 0) >= lax.broadcasted_iota(
        jnp.int32, (tokens, tokens), 1
    )
    for head in range(heads):
        query = rotate(total(head * tokens, tokens) * inverse, cosine, sine)
        scores = lax.dot_general(
            query, key, (((1,), (1,)), ((), ())),
            precision=lax.Precision.HIGHEST, preferred_element_type=jnp.float32,
        ) * (1.0 / np.sqrt(np.float32(HD)))
        expo = jnp.where(causal, jnp.exp(scores), 0.0)
        weights = (expo / jnp.sum(expo, axis=1, keepdims=True)).astype(jnp.bfloat16)
        mixed = jnp.dot(weights, value, preferred_element_type=jnp.float32).astype(jnp.bfloat16)
        for dest in range(NZ):
            out_ref[dest, head * tokens : (head + 1) * tokens, :] = mixed


def output_kernel(y_ref, heads_ref, o_mine, o_part, hidden_ref, base_ref, *refs):
    sent = refs[: NY - 1]
    joined, pieces = refs[NY - 1 :]
    tokens, width = hidden_ref.shape[1:]
    for source in range(heads_ref.shape[0]):
        for head in range(heads_ref.shape[1] // tokens):
            at = (source * (heads_ref.shape[1] // tokens) + head) * HD
            joined[:, at : at + HD] = heads_ref[source, head * tokens : (head + 1) * tokens, :]
    for half, weight in enumerate((o_mine, o_part)):
        for pair in range(NY // 2):
            at = pair * 2 * width
            product = jnp.dot(
                joined[...], weight[:, at : at + 2 * width], preferred_element_type=jnp.float32
            )
            for inner in range(2):
                step = lax.rem(pair * 2 + inner + NY - y_ref[0], NY)
                pieces[step, half] = product[:, inner * width : (inner + 1) * width]
    base_ref[...] = hidden_ref[...].astype(jnp.float32) + pieces[0]
    for k in range(1, NY):
        sent[k - 1][...] = pieces[k].astype(jnp.bfloat16)


VMEM = pl.BlockSpec(memory_space=pltpu.VMEM)
SMEM = pl.BlockSpec(memory_space=pltpu.SMEM)


def summed_over(value, axis, steps):
    count = lax.axis_size(axis)
    got = [
        lax.ppermute(value, axis, [(i, i ^ step) for i in range(count)]) for step in steps
    ]
    if len(got) == 1:
        return value + got[0]
    return (value + got[0]) + (got[1] + got[2])


def local(inputs, target, norm_gains, w_query, w_keyval, w_output, noise_seed, step_count):
    section = lax.axis_index("section")
    sections = lax.axis_size("section")
    y = lax.axis_index("y")
    z = lax.axis_index("z")
    core = lax.axis_index("core")
    tokens, width = inputs.shape
    full = width * NY * NZ * NC
    query_cols = w_query.shape[3]
    keyval_cols = w_keyval.shape[3]
    block = z * NC + core
    amount = jnp.where(core == 0, perturb_scale, -perturb_scale).astype(jnp.float32)
    spread = NZ * NC * width

    def salt(code):
        return mix_bits(mix_bits(step_count[0] * 40503 + (4 * section + code) * 1000003) ^ noise_seed[0])

    wq, wk, wo = w_query[0, 0], w_keyval[0, 0], w_output[0, 0]
    paired = jax.ShapeDtypeStruct((wq.shape[0], query_cols + keyval_cols), jnp.bfloat16)
    zq, zk, in_mine, in_other = pl.pallas_call(
        functools.partial(perturb_input_kernel, full, spread, NY),
        grid=(NY,),
        in_specs=[SMEM, SMEM, by_rows(wq, NY), by_rows(wk, NY)],
        out_specs=[by_rows(wq, NY), by_rows(wk, NY), by_rows(paired, NY), by_rows(paired, NY)],
        out_shape=[
            jax.ShapeDtypeStruct(wq.shape, jnp.float32),
            jax.ShapeDtypeStruct(wk.shape, jnp.float32),
            paired,
            paired,
        ],
        compiler_params=limit(14),
        cost_estimate=noise_cost(wq.size + wk.size),
    )(
        jnp.stack([salt(1), salt(2), block * width, y * query_cols, y * keyval_cols]),
        amount.reshape(1), wq, wk,
    )
    in_part = swapped(in_other)
    hidden = jnp.stack([inputs, swapped(inputs)])
    around = [hidden] + [shifted(hidden, "y", NY, k) for k in range(1, NY)]
    wo, around[1] = lax.optimization_barrier((wo, around[1]))
    zo, o_mine, o_other = pl.pallas_call(
        functools.partial(perturb_output_kernel, full, spread, width),
        grid=(8,),
        in_specs=[SMEM, SMEM, by_rows(wo, 8)],
        out_specs=[by_rows(wo, 8)] * 3,
        out_shape=[
            jax.ShapeDtypeStruct(wo.shape, jnp.float32),
            jax.ShapeDtypeStruct(wo.shape, jnp.bfloat16),
            jax.ShapeDtypeStruct(wo.shape, jnp.bfloat16),
        ],
        compiler_params=limit(14),
        cost_estimate=noise_cost(wo.size),
    )(
        jnp.stack([salt(3), y * query_cols, block * width]),
        amount.reshape(1), wo,
    )
    o_part = swapped(o_other)
    in_mine, o_mine = lax.optimization_barrier((in_mine, o_mine))

    gain_noise = noise_of(jnp.arange(full, dtype=jnp.int32), salt(0))
    gains = (norm_gains[0] + amount * gain_noise).reshape(NY, NZ, NC, width)
    gains = lax.dynamic_index_in_dim(gains, z, 1, keepdims=False)
    gains = jnp.where(core == 0, gains, gains[:, ::-1])
    gains = jnp.take(gains.transpose(1, 0, 2), (y - jnp.arange(NY)) % NY, axis=1)

    cosine, sine = (jnp.asarray(t) for t in rope_tables(tokens))
    place = y.reshape(1)
    heads_z = query_cols // HD // NZ
    rows = (heads_z + 2) * tokens + 16

    def project(around):
        return pl.pallas_call(
            project_kernel,
            in_specs=[SMEM] + [VMEM] * (NY + 3),
            out_specs=VMEM,
            out_shape=jax.ShapeDtypeStruct((NZ, rows, HD), jnp.bfloat16),
            scratch_shapes=[pltpu.VMEM((NC, tokens, NY * width), jnp.bfloat16)],
            compiler_params=limit(14),
        )(place, *around, gains, in_mine, in_part)

    def attend(received):
        return pl.pallas_call(
            functools.partial(attend_kernel, full),
            in_specs=[VMEM] * 3,
            out_specs=VMEM,
            out_shape=jax.ShapeDtypeStruct((NZ, heads_z * tokens, HD), jnp.bfloat16),
            compiler_params=limit(14),
        )(received, cosine, sine)

    def output(heads, hidden):
        return pl.pallas_call(
            output_kernel,
            in_specs=[SMEM] + [VMEM] * 4,
            out_specs=[VMEM] * NY,
            out_shape=[jax.ShapeDtypeStruct(hidden.shape, jnp.float32)]
            + [jax.ShapeDtypeStruct(hidden.shape, jnp.bfloat16)] * (NY - 1),
            scratch_shapes=[
                pltpu.VMEM((tokens, query_cols), jnp.bfloat16),
                pltpu.VMEM((NY,) + hidden.shape, jnp.float32),
            ],
            compiler_params=limit(14),
        )(place, heads, o_mine, o_part, hidden)

    goal = jnp.stack([target, swapped(target)])
    record = jnp.zeros_like(hidden)
    for tick in range(4):
        if tick:
            around = [hidden] + [shifted(hidden, "y", NY, k) for k in range(1, NY)]
        received = lax.all_to_all(project(around), "z", 0, 0, tiled=True)
        heads = lax.all_to_all(attend(received), "z", 0, 0, tiled=True)
        base, *pieces = output(heads, hidden)
        for k in range(1, NY):
            base = base + shifted(pieces[k - 1], "y", NY, k).astype(jnp.float32)
        result = base.astype(jnp.bfloat16)
        record = jnp.where(section == tick, result, record)
        if tick < 3:
            hidden = lax.ppermute(result, "section", [(tick, tick + 1)])

    gap = result.astype(jnp.float32) - goal.astype(jnp.float32)
    squared = jnp.sum(gap * gap)
    squared = jnp.full((8, LANE), squared)
    squared = summed_over(squared, "y", (1, 2, 3))
    squared = summed_over(squared, "z", (1,))
    squared = summed_over(squared, "z", (2, 4, 6))
    copies = [lax.ppermute(squared, "section", [(sections - 1, k)]) for k in range(sections - 1)]
    squared = jnp.where(section == sections - 1, squared, sum(copies[1:], copies[0]))
    partner = swapped(squared)
    squared = jnp.where(core == 0, jnp.stack([squared, partner]), jnp.stack([partner, squared]))[:, 0, 0]
    losses = squared / (tokens * full)
    rate = learn_rate * ((losses[0] - losses[1]) / (2.0 * perturb_scale))
    new_gains = (norm_gains[0] - rate * gain_noise)[None]

    arrays = (wq, wk, wo)
    specs = [by_rows(w, 8) for w in arrays]
    new_query, new_keyval, new_output = pl.pallas_call(
        update_kernel,
        grid=(8,),
        in_specs=[SMEM] + specs + specs,
        out_specs=specs,
        out_shape=[jax.ShapeDtypeStruct(w.shape, jnp.bfloat16) for w in arrays],
        compiler_params=limit(14),
    )(rate.reshape(1), *arrays, zq, zk, zo)
    mine, other = record[0], swapped(record[1])
    layer_outputs = jnp.where(core == 0, jnp.stack([mine, other]), jnp.stack([other, mine]))[None]
    return (
        layer_outputs,
        losses[None],
        new_gains,
        new_query[None, None],
        new_keyval[None, None],
        new_output[None, None],
    )


def solution(mesh):
    mesh = Mesh(mesh.devices.reshape(-1, NY, NZ, NC), ("section", "y", "z", "core"))
    tensor = ("y", "z", "core")
    return jax.shard_map(
        local,
        mesh=mesh,
        in_specs=(
            P(None, tensor),
            P(None, tensor),
            P("section", None),
            P("section", tensor, None, None),
            P("section", tensor, None, None),
            P("section", tensor, None, None),
            P(),
            P(),
        ),
        out_specs=(
            P("section", None, None, tensor),
            P("section", None),
            P("section", None),
            P("section", tensor, None, None),
            P("section", tensor, None, None),
            P("section", tensor, None, None),
        ),
        check_vma=False,
    )
```

```python
import functools

import jax
import jax.numpy as jnp
import numpy as np
from jax import lax
from jax.experimental import pallas as pl
from jax.experimental.pallas import tpu as pltpu
from jax.sharding import Mesh, PartitionSpec as P

HD = 128
NY, NZ, NC = 4, 8, 2
LANE = 128

perturb_scale = 0.001
learn_rate = 1e-05
rope_base = 500000.0


def logical(value, by):
    return lax.shift_right_logical(value, jnp.full(value.shape, by, value.dtype))


def mix_bits(hashed):
    hashed = hashed ^ logical(hashed, 16)
    hashed = hashed * jnp.int32(2146121005)
    hashed = hashed ^ logical(hashed, 15)
    hashed = hashed * jnp.int32(-2073254261)
    hashed = hashed ^ logical(hashed, 16)
    return hashed


def noise_of(index, salt):
    hashed = mix_bits(mix_bits(index ^ salt) + salt)
    uniform_part = logical(hashed, 8).astype(jnp.float32) * (1.0 / 16777216.0)
    return (uniform_part - 0.5) * 3.4641016


def limit(mib):
    return pltpu.CompilerParams(vmem_limit_bytes=mib * 1024 * 1024)


def perturb_input_kernel(full, spread, groups, ints_ref, sign_ref, q_ref, k_ref, zq_ref, zk_ref, mine_ref, other_ref):
    rows, query_cols = q_ref.shape
    keyval_cols = k_ref.shape[1]
    row = lax.broadcasted_iota(jnp.int32, (rows, 1), 0) + pl.program_id(0) * spread + ints_ref[2]
    for w_ref, z_ref, at, salt, cols, first in (
        (q_ref, zq_ref, 0, ints_ref[0], full, ints_ref[3]),
        (k_ref, zk_ref, query_cols, ints_ref[1], keyval_cols * groups, ints_ref[4]),
    ):
        width = w_ref.shape[1]
        col = lax.broadcasted_iota(jnp.int32, (1, width), 1) + first
        z = noise_of(row * cols + col, salt)
        z_ref[...] = z
        w = w_ref[...].astype(jnp.float32)
        shift = sign_ref[0] * z
        mine_ref[:, at : at + width] = (w + shift).astype(jnp.bfloat16)
        other_ref[:, at : at + width] = (w - shift).astype(jnp.bfloat16)


def perturb_output_kernel(full, spread, width, ints_ref, sign_ref, w_ref, z_ref, mine_ref, other_ref):
    rows, cols = w_ref.shape
    row = lax.broadcasted_iota(jnp.int32, (rows, 1), 0) + pl.program_id(0) * rows + ints_ref[1]
    col = lax.broadcasted_iota(jnp.int32, (1, cols), 1)
    col = col + col // width * (spread - width) + ints_ref[2]
    z = noise_of(row * full + col, ints_ref[0])
    z_ref[...] = z
    w = w_ref[...].astype(jnp.float32)
    shift = sign_ref[0] * z
    mine_ref[...] = (w + shift).astype(jnp.bfloat16)
    other_ref[...] = (w - shift).astype(jnp.bfloat16)


def update_kernel(entries, sums_ref, *refs):
    rate = learn_rate * ((sums_ref[0] / entries - sums_ref[1] / entries) / (2.0 * perturb_scale))
    count = len(refs) // 3
    for w_ref, z_ref, out_ref in zip(refs[:count], refs[count : 2 * count], refs[2 * count :]):
        out_ref[...] = (w_ref[...].astype(jnp.float32) - rate * z_ref[...]).astype(jnp.bfloat16)


def in_hbm(array):
    return pltpu.with_memory_space_constraint(array, pltpu.HBM)


def by_rows(array, steps):
    return pl.BlockSpec((array.shape[0] // steps, array.shape[1]), lambda i: (i, 0))


def noise_cost(count):
    return pl.CostEstimate(flops=60 * count, bytes_accessed=10 * count, transcendentals=0)


def shifted(array, axis, count, by):
    return lax.ppermute(array, axis, [(i, (i + by) % count) for i in range(count)])


def swapped(array):
    return lax.ppermute(array, "core", [(0, 1), (1, 0)])


def rope_tables(tokens):
    half = HD // 2
    frequency = np.float32(rope_base) ** (-np.arange(half, dtype=np.float32) * np.float32(2.0) / np.float32(HD))
    angles = np.arange(tokens, dtype=np.float32)[:, None] * frequency.astype(np.float32)[None, :]
    cosine = np.cos(angles.astype(np.float64)).astype(np.float32)
    sine = np.sin(angles.astype(np.float64)).astype(np.float32)
    return np.concatenate([cosine, cosine], 1), np.concatenate([-sine, sine], 1)


def rotate(values, cosine, sine):
    return values * cosine + pltpu.roll(values, HD // 2, 1) * sine


def same_index(size):
    return lax.broadcasted_iota(jnp.int32, (size, size), 0) == lax.broadcasted_iota(
        jnp.int32, (size, size), 1
    )


def project_kernel(y_ref, *refs):
    around = refs[:NY]
    gains_ref, mine, part, out_ref, scaled = refs[NY:]
    tokens, width = around[0].shape[1:]
    total = jnp.zeros((tokens, 1), jnp.float32)
    for k in range(NY):
        place = pl.multiple_of(lax.rem(y_ref[0] + (NY - k), NY) * width, width)
        for half in range(NC):
            wide = around[k][half].astype(jnp.float32)
            total = total + jnp.sum(wide * wide, axis=1, keepdims=True)
            scaled[half, :, pl.ds(place, width)] = (wide * gains_ref[half, k : k + 1, :]).astype(jnp.bfloat16)

    def product(start, size):
        return jnp.dot(
            scaled[0], mine[:, start : start + size], preferred_element_type=jnp.float32
        ) + jnp.dot(scaled[1], part[:, start : start + size], preferred_element_type=jnp.float32)

    kept = out_ref.shape[1] - 16 - 2 * tokens
    span = kept // tokens * HD
    for dest in range(NZ):
        query = product(dest * span, span).astype(jnp.bfloat16)
        for head in range(span // HD):
            out_ref[dest, head * tokens : (head + 1) * tokens, :] = query[:, head * HD : (head + 1) * HD]
    groups = (mine.shape[1] - NZ * span) // (2 * HD)
    for group in range(groups):
        keyval = product(NZ * span + group * 2 * HD, 2 * HD).astype(jnp.bfloat16)
        for dest in range(group * NZ // groups, (group + 1) * NZ // groups):
            out_ref[dest, kept : kept + tokens, :] = keyval[:, :HD]
            out_ref[dest, kept + tokens : kept + 2 * tokens, :] = keyval[:, HD:]
    row = jnp.sum(jnp.where(same_index(tokens), total, 0.0), axis=0, keepdims=True)
    high = row.astype(jnp.bfloat16).astype(jnp.float32)
    line = lax.broadcasted_iota(jnp.int32, (16, tokens), 0)
    extra = jnp.where(line == 0, high, jnp.where(line == 1, row - high, 0.0)).astype(jnp.bfloat16)
    for dest in range(NZ):
        out_ref[dest, kept + 2 * tokens :, :] = extra


def attend_kernel(full, recv_ref, cos_ref, sin_ref, out_ref):
    tokens = cos_ref.shape[0]
    heads = out_ref.shape[1] // tokens

    def total(start, size):
        acc = recv_ref[0, start : start + size, :].astype(jnp.float32)
        for source in range(1, NZ):
            acc = acc + recv_ref[source, start : start + size, :].astype(jnp.float32)
        return acc

    cosine = cos_ref[...]
    sine = sin_ref[...]
    kept = heads * tokens
    squares = total(kept + 2 * tokens, 16)
    row = squares[0:1] + squares[1:2]
    column = jnp.sum(jnp.where(same_index(tokens), row, 0.0), axis=1, keepdims=True)
    inverse = lax.rsqrt(column / full + 1e-05)
    key = (total(kept, tokens) * inverse).astype(jnp.bfloat16).astype(jnp.float32)
    key = rotate(key, cosine, sine)
    value = (total(kept + tokens, tokens) * inverse).astype(jnp.bfloat16)
    causal = lax.broadcasted_iota(jnp.int32, (tokens, tokens), 0) >= lax.broadcasted_iota(
        jnp.int32, (tokens, tokens), 1
    )
    for head in range(heads):
        query = rotate(total(head * tokens, tokens) * inverse, cosine, sine)
        scores = lax.dot_general(
            query, key, (((1,), (1,)), ((), ())),
            precision=lax.Precision.HIGHEST, preferred_element_type=jnp.float32,
        ) * (1.0 / np.sqrt(np.float32(HD)))
        expo = jnp.where(causal, jnp.exp(scores), 0.0)
        weights = (expo / jnp.sum(expo, axis=1, keepdims=True)).astype(jnp.bfloat16)
        mixed = jnp.dot(weights, value, preferred_element_type=jnp.float32).astype(jnp.bfloat16)
        for dest in range(NZ):
            out_ref[dest, head * tokens : (head + 1) * tokens, :] = mixed


def output_kernel(y_ref, heads_ref, o_mine, o_part, hidden_ref, base_ref, *refs):
    sent = refs[: NY - 1]
    joined, pieces = refs[NY - 1 :]
    tokens, width = hidden_ref.shape[1:]
    for source in range(heads_ref.shape[0]):
        for head in range(heads_ref.shape[1] // tokens):
            at = (source * (heads_ref.shape[1] // tokens) + head) * HD
            joined[:, at : at + HD] = heads_ref[source, head * tokens : (head + 1) * tokens, :]
    for half, weight in enumerate((o_mine, o_part)):
        for pair in range(NY // 2):
            at = pair * 2 * width
            product = jnp.dot(
                joined[...], weight[:, at : at + 2 * width], preferred_element_type=jnp.float32
            )
            for inner in range(2):
                step = lax.rem(pair * 2 + inner + NY - y_ref[0], NY)
                pieces[step, half] = product[:, inner * width : (inner + 1) * width]
    base_ref[...] = hidden_ref[...].astype(jnp.float32) + pieces[0]
    for k in range(1, NY):
        sent[k - 1][...] = pieces[k].astype(jnp.bfloat16)


VMEM = pl.BlockSpec(memory_space=pltpu.VMEM)
SMEM = pl.BlockSpec(memory_space=pltpu.SMEM)


def summed_over(value, axis, steps):
    count = lax.axis_size(axis)
    got = [
        lax.ppermute(value, axis, [(i, i ^ step) for i in range(count)]) for step in steps
    ]
    if len(got) == 1:
        return value + got[0]
    return (value + got[0]) + (got[1] + got[2])


def local(inputs, target, norm_gains, w_query, w_keyval, w_output, noise_seed, step_count):
    section = lax.axis_index("section")
    sections = lax.axis_size("section")
    y = lax.axis_index("y")
    z = lax.axis_index("z")
    core = lax.axis_index("core")
    tokens, width = inputs.shape
    full = width * NY * NZ * NC
    query_cols = w_query.shape[3]
    keyval_cols = w_keyval.shape[3]
    block = z * NC + core
    amount = jnp.where(core == 0, perturb_scale, -perturb_scale).astype(jnp.float32)
    spread = NZ * NC * width

    def salt(code):
        return mix_bits(mix_bits(step_count[0] * 40503 + (4 * section + code) * 1000003) ^ noise_seed[0])

    gain_noise = noise_of(jnp.arange(full, dtype=jnp.int32), salt(0))
    gains = (norm_gains[0] + amount * gain_noise).reshape(NY, NZ, NC, width)
    gains = lax.dynamic_index_in_dim(gains, z, 1, keepdims=False)
    gains = jnp.where(core == 0, gains, gains[:, ::-1])
    gains = gains.transpose(1, 0, 2)
    gains = jnp.concatenate([gains, gains], axis=1)[:, ::-1]
    gains = lax.dynamic_slice_in_dim(gains, NY - 1 - y, NY, 1)

    wq, wk, wo = w_query[0, 0], w_keyval[0, 0], w_output[0, 0]
    ints = jnp.stack([salt(1), salt(2), block * width, y * query_cols, y * keyval_cols])
    ints_out = jnp.stack([salt(3), y * query_cols, block * width])
    gains, ints, ints_out, gain_noise = lax.optimization_barrier((gains, ints, ints_out, gain_noise))
    paired = jax.ShapeDtypeStruct((wq.shape[0], query_cols + keyval_cols), jnp.bfloat16)
    zq, zk, in_mine, in_other = pl.pallas_call(
        functools.partial(perturb_input_kernel, full, spread, NY),
        grid=(NY,),
        in_specs=[SMEM, SMEM, by_rows(wq, NY), by_rows(wk, NY)],
        out_specs=[by_rows(wq, NY), by_rows(wk, NY), by_rows(paired, NY), by_rows(paired, NY)],
        out_shape=[
            pltpu.HBM(wq.shape, jnp.float32),
            pltpu.HBM(wk.shape, jnp.float32),
            paired,
            paired,
        ],
        compiler_params=limit(14),
        cost_estimate=noise_cost(wq.size + wk.size),
    )(
        ints,
        amount.reshape(1), in_hbm(wq), in_hbm(wk),
    )
    in_part = swapped(in_other)
    hidden = jnp.stack([inputs, swapped(inputs)])
    around = [hidden] + [shifted(hidden, "y", NY, k) for k in range(1, NY)]
    wo, around[1] = lax.optimization_barrier((wo, around[1]))
    zo, o_mine, o_other = pl.pallas_call(
        functools.partial(perturb_output_kernel, full, spread, width),
        grid=(8,),
        in_specs=[SMEM, SMEM, by_rows(wo, 8)],
        out_specs=[by_rows(wo, 8)] * 3,
        out_shape=[
            pltpu.HBM(wo.shape, jnp.float32),
            jax.ShapeDtypeStruct(wo.shape, jnp.bfloat16),
            jax.ShapeDtypeStruct(wo.shape, jnp.bfloat16),
        ],
        compiler_params=limit(14),
        cost_estimate=noise_cost(wo.size),
    )(
        ints_out,
        amount.reshape(1), in_hbm(wo),
    )
    o_part = swapped(o_other)
    in_mine, in_part, o_mine, o_part = lax.optimization_barrier((in_mine, in_part, o_mine, o_part))

    cosine, sine = (jnp.asarray(t) for t in rope_tables(tokens))
    place = y.reshape(1)
    heads_z = query_cols // HD // NZ
    rows = (heads_z + 2) * tokens + 16

    def project(around):
        return pl.pallas_call(
            project_kernel,
            in_specs=[SMEM] + [VMEM] * (NY + 3),
            out_specs=VMEM,
            out_shape=jax.ShapeDtypeStruct((NZ, rows, HD), jnp.bfloat16),
            scratch_shapes=[pltpu.VMEM((NC, tokens, NY * width), jnp.bfloat16)],
            compiler_params=limit(14),
        )(place, *around, gains, in_mine, in_part)

    def attend(received):
        return pl.pallas_call(
            functools.partial(attend_kernel, full),
            in_specs=[VMEM] * 3,
            out_specs=VMEM,
            out_shape=jax.ShapeDtypeStruct((NZ, heads_z * tokens, HD), jnp.bfloat16),
            compiler_params=limit(14),
        )(received, cosine, sine)

    def output(heads, hidden):
        return pl.pallas_call(
            output_kernel,
            in_specs=[SMEM] + [VMEM] * 4,
            out_specs=[VMEM] * NY,
            out_shape=[jax.ShapeDtypeStruct(hidden.shape, jnp.float32)]
            + [jax.ShapeDtypeStruct(hidden.shape, jnp.bfloat16)] * (NY - 1),
            scratch_shapes=[
                pltpu.VMEM((tokens, query_cols), jnp.bfloat16),
                pltpu.VMEM((NY,) + hidden.shape, jnp.float32),
            ],
            compiler_params=limit(14),
        )(place, heads, o_mine, o_part, hidden)

    goal = jnp.stack([target, swapped(target)])
    record = jnp.zeros_like(hidden)
    for tick in range(4):
        if tick:
            around = [hidden] + [shifted(hidden, "y", NY, k) for k in range(1, NY)]
        received = lax.all_to_all(project(around), "z", 0, 0, tiled=True)
        heads = lax.all_to_all(attend(received), "z", 0, 0, tiled=True)
        base, *pieces = output(heads, hidden)
        for k in range(1, NY):
            base = base + shifted(pieces[k - 1], "y", NY, k).astype(jnp.float32)
        result = base.astype(jnp.bfloat16)
        record = jnp.where(section == tick, result, record)
        if tick < 3:
            hidden = lax.ppermute(result, "section", [(tick, tick + 1)])

    gap = result.astype(jnp.float32) - goal.astype(jnp.float32)
    squared = jnp.sum(gap * gap)
    squared = jnp.full((8, LANE), squared)
    squared = summed_over(squared, "y", (1, 2, 3))
    squared = summed_over(squared, "z", (1,))
    squared = summed_over(squared, "z", (2, 4, 6))
    copies = [lax.ppermute(squared, "section", [(sections - 1, k)]) for k in range(sections - 1)]
    squared = jnp.where(section == sections - 1, squared, sum(copies[1:], copies[0]))
    partner = swapped(squared)
    squared = jnp.where(core == 0, jnp.stack([squared, partner]), jnp.stack([partner, squared]))[:, 0, 0]
    losses = squared / (tokens * full)
    rate = learn_rate * ((losses[0] - losses[1]) / (2.0 * perturb_scale))
    new_gains = (norm_gains[0] - rate * gain_noise)[None]

    arrays = (wq, wk, wo)
    specs = [by_rows(w, 8) for w in arrays]
    new_query, new_keyval, new_output = pl.pallas_call(
        functools.partial(update_kernel, float(tokens * full)),
        grid=(8,),
        in_specs=[SMEM] + specs + specs,
        out_specs=specs,
        out_shape=[pltpu.HBM(w.shape, jnp.bfloat16) for w in arrays],
        compiler_params=limit(14),
    )(squared, *map(in_hbm, (*arrays, zq, zk, zo)))
    mine, other = record[0], swapped(record[1])
    layer_outputs = jnp.where(core == 0, jnp.stack([mine, other]), jnp.stack([other, mine]))[None]
    return (
        layer_outputs,
        losses[None],
        new_gains,
        new_query[None, None],
        new_keyval[None, None],
        new_output[None, None],
    )


def solution(mesh):
    mesh = Mesh(mesh.devices.reshape(-1, NY, NZ, NC), ("section", "y", "z", "core"))
    tensor = ("y", "z", "core")
    return jax.shard_map(
        local,
        mesh=mesh,
        in_specs=(
            P(None, tensor),
            P(None, tensor),
            P("section", None),
            P("section", tensor, None, None),
            P("section", tensor, None, None),
            P("section", tensor, None, None),
            P(),
            P(),
        ),
        out_specs=(
            P("section", None, None, tensor),
            P("section", None),
            P("section", None),
            P("section", tensor, None, None),
            P("section", tensor, None, None),
            P("section", tensor, None, None),
        ),
        check_vma=False,
    )
```

```python
import functools

import jax
import jax.numpy as jnp
import numpy as np
from jax import lax
from jax.experimental import pallas as pl
from jax.experimental.pallas import tpu as pltpu
from jax.sharding import Mesh, PartitionSpec as P

HD = 128
NY, NZ, NC = 4, 8, 2
LANE = 128

perturb_scale = 0.001
learn_rate = 1e-05
rope_base = 500000.0


def logical(value, by):
    return lax.shift_right_logical(value, jnp.full(value.shape, by, value.dtype))


def mix_bits(hashed):
    hashed = hashed ^ logical(hashed, 16)
    hashed = hashed * jnp.int32(2146121005)
    hashed = hashed ^ logical(hashed, 15)
    hashed = hashed * jnp.int32(-2073254261)
    hashed = hashed ^ logical(hashed, 16)
    return hashed


def noise_of(index, salt):
    hashed = mix_bits(mix_bits(index ^ salt) + salt)
    return logical(hashed, 8).astype(jnp.float32) * (3.4641016 / 16777216.0) - 0.5 * 3.4641016


def limit(mib):
    return pltpu.CompilerParams(vmem_limit_bytes=mib * 1024 * 1024)


def perturb_input_kernel(full, spread, groups, ints_ref, sign_ref, q_ref, k_ref, zq_ref, zk_ref, mine_ref, other_ref):
    rows, query_cols = q_ref.shape
    keyval_cols = k_ref.shape[1]
    row = lax.broadcasted_iota(jnp.int32, (rows, 1), 0) + pl.program_id(0) * spread + ints_ref[2]
    for w_ref, z_ref, at, salt, cols, first in (
        (q_ref, zq_ref, 0, ints_ref[0], full, ints_ref[3]),
        (k_ref, zk_ref, query_cols, ints_ref[1], keyval_cols * groups, ints_ref[4]),
    ):
        width = w_ref.shape[1]
        col = lax.broadcasted_iota(jnp.int32, (1, width), 1) + first
        z = noise_of(row * cols + col, salt)
        z_ref[...] = z.astype(jnp.bfloat16)
        w = w_ref[...].astype(jnp.float32)
        shift = sign_ref[0] * z
        mine_ref[:, at : at + width] = (w + shift).astype(jnp.bfloat16)
        other_ref[:, at : at + width] = (w - shift).astype(jnp.bfloat16)


def perturb_output_kernel(full, spread, width, ints_ref, sign_ref, w_ref, z_ref, mine_ref, other_ref):
    rows, cols = w_ref.shape
    row = lax.broadcasted_iota(jnp.int32, (rows, 1), 0) + pl.program_id(0) * rows + ints_ref[1]
    col = lax.broadcasted_iota(jnp.int32, (1, cols), 1)
    col = col + col // width * (spread - width) + ints_ref[2]
    z = noise_of(row * full + col, ints_ref[0])
    z_ref[...] = z.astype(jnp.bfloat16)
    w = w_ref[...].astype(jnp.float32)
    shift = sign_ref[0] * z
    mine_ref[...] = (w + shift).astype(jnp.bfloat16)
    other_ref[...] = (w - shift).astype(jnp.bfloat16)


def finish_kernel(base_ref, *refs):
    pieces = refs[: NY - 1]
    goal_ref, result_ref, gap_ref = refs[NY - 1 :]
    total = jnp.zeros(gap_ref.shape, jnp.float32)
    for half in range(NC):
        summed = base_ref[half]
        for piece in pieces:
            summed = summed + piece[half].astype(jnp.float32)
        result = summed.astype(jnp.bfloat16)
        result_ref[half] = result
        gap = result.astype(jnp.float32) - goal_ref[half].astype(jnp.float32)
        total = total + jnp.sum((gap * gap).reshape((-1,) + gap_ref.shape), axis=0)
    gap_ref[...] = total


def update_kernel(entries, core_ref, own_ref, partner_ref, gain_ref, noise_ref, *refs):
    rate_ref = refs[-1]
    loss_ref, new_gain_ref = refs[-3], refs[-2]
    refs = refs[:-3]

    @pl.when(pl.program_id(0) == 0)
    def _():
        own = jnp.sum(own_ref[...]) / entries
        partner = jnp.sum(partner_ref[...]) / entries
        first = core_ref[0] == 0
        plus = jnp.where(first, own, partner)
        minus = jnp.where(first, partner, own)
        loss_ref[0, 0] = plus
        loss_ref[0, 1] = minus
        rate_ref[0] = learn_rate * ((plus - minus) / (2.0 * perturb_scale))
        new_gain_ref[...] = gain_ref[...] - rate_ref[0] * noise_ref[...]

    rate = rate_ref[0]
    count = len(refs) // 3
    for w_ref, z_ref, out_ref in zip(refs[:count], refs[count : 2 * count], refs[2 * count :]):
        out_ref[...] = (w_ref[...].astype(jnp.float32) - rate * z_ref[...].astype(jnp.float32)).astype(jnp.bfloat16)


def in_hbm(array):
    return pltpu.with_memory_space_constraint(array, pltpu.HBM)


def by_rows(array, steps):
    return pl.BlockSpec((array.shape[0] // steps, array.shape[1]), lambda i: (i, 0))


def noise_cost(count):
    return pl.CostEstimate(flops=60 * count, bytes_accessed=10 * count, transcendentals=0)


def shifted(array, axis, count, by):
    return lax.ppermute(array, axis, [(i, (i + by) % count) for i in range(count)])


def swapped(array):
    return lax.ppermute(array, "core", [(0, 1), (1, 0)])


def rope_tables(tokens):
    half = HD // 2
    frequency = np.float32(rope_base) ** (-np.arange(half, dtype=np.float32) * np.float32(2.0) / np.float32(HD))
    angles = np.arange(tokens, dtype=np.float32)[:, None] * frequency.astype(np.float32)[None, :]
    cosine = np.cos(angles.astype(np.float64)).astype(np.float32)
    sine = np.sin(angles.astype(np.float64)).astype(np.float32)
    return np.concatenate([cosine, cosine], 1), np.concatenate([-sine, sine], 1)


def rotate(values, cosine, sine):
    return values * cosine + pltpu.roll(values, HD // 2, 1) * sine


def same_index(size):
    return lax.broadcasted_iota(jnp.int32, (size, size), 0) == lax.broadcasted_iota(
        jnp.int32, (size, size), 1
    )


def project_kernel(y_ref, *refs):
    around = refs[:NY]
    gains_ref, mine, part, out_ref, scaled = refs[NY:]
    tokens, width = around[0].shape[1:]
    total = jnp.zeros((tokens, 1), jnp.float32)
    for k in range(NY):
        place = pl.multiple_of(lax.rem(y_ref[0] + (NY - k), NY) * width, width)
        for half in range(NC):
            wide = around[k][half].astype(jnp.float32)
            total = total + jnp.sum(wide * wide, axis=1, keepdims=True)
            scaled[half, :, pl.ds(place, width)] = (wide * gains_ref[half, k : k + 1, :]).astype(jnp.bfloat16)

    def product(start, size):
        return jnp.dot(
            scaled[0], mine[:, start : start + size], preferred_element_type=jnp.float32
        ) + jnp.dot(scaled[1], part[:, start : start + size], preferred_element_type=jnp.float32)

    kept = out_ref.shape[1] - 16 - 2 * tokens
    span = kept // tokens * HD
    for dest in range(NZ):
        query = product(dest * span, span).astype(jnp.bfloat16)
        for head in range(span // HD):
            out_ref[dest, head * tokens : (head + 1) * tokens, :] = query[:, head * HD : (head + 1) * HD]
    groups = (mine.shape[1] - NZ * span) // (2 * HD)
    for group in range(groups):
        keyval = product(NZ * span + group * 2 * HD, 2 * HD).astype(jnp.bfloat16)
        for dest in range(group * NZ // groups, (group + 1) * NZ // groups):
            out_ref[dest, kept : kept + tokens, :] = keyval[:, :HD]
            out_ref[dest, kept + tokens : kept + 2 * tokens, :] = keyval[:, HD:]
    row = jnp.sum(jnp.where(same_index(tokens), total, 0.0), axis=0, keepdims=True)
    high = row.astype(jnp.bfloat16).astype(jnp.float32)
    line = lax.broadcasted_iota(jnp.int32, (16, tokens), 0)
    extra = jnp.where(line == 0, high, jnp.where(line == 1, row - high, 0.0)).astype(jnp.bfloat16)
    for dest in range(NZ):
        out_ref[dest, kept + 2 * tokens :, :] = extra


def attend_kernel(full, recv_ref, cos_ref, sin_ref, out_ref):
    tokens = cos_ref.shape[0]
    heads = out_ref.shape[1] // tokens

    def total(start, size):
        acc = recv_ref[0, start : start + size, :].astype(jnp.float32)
        for source in range(1, NZ):
            acc = acc + recv_ref[source, start : start + size, :].astype(jnp.float32)
        return acc

    cosine = cos_ref[...]
    sine = sin_ref[...]
    kept = heads * tokens
    squares = total(kept + 2 * tokens, 16)
    row = squares[0:1] + squares[1:2]
    column = jnp.sum(jnp.where(same_index(tokens), row, 0.0), axis=1, keepdims=True)
    inverse = lax.rsqrt(column / full + 1e-05)
    key = (total(kept, tokens) * inverse).astype(jnp.bfloat16).astype(jnp.float32)
    key = rotate(key, cosine, sine)
    value = (total(kept + tokens, tokens) * inverse).astype(jnp.bfloat16)
    causal = lax.broadcasted_iota(jnp.int32, (tokens, tokens), 0) >= lax.broadcasted_iota(
        jnp.int32, (tokens, tokens), 1
    )
    for head in range(heads):
        query = rotate(total(head * tokens, tokens) * inverse, cosine, sine)
        scores = lax.dot_general(
            query, key, (((1,), (1,)), ((), ())),
            precision=lax.Precision.HIGHEST, preferred_element_type=jnp.float32,
        ) * (1.0 / np.sqrt(np.float32(HD)))
        expo = jnp.where(causal, jnp.exp(scores), 0.0)
        weights = (expo / jnp.sum(expo, axis=1, keepdims=True)).astype(jnp.bfloat16)
        mixed = jnp.dot(weights, value, preferred_element_type=jnp.float32).astype(jnp.bfloat16)
        for dest in range(NZ):
            out_ref[dest, head * tokens : (head + 1) * tokens, :] = mixed


def output_kernel(y_ref, heads_ref, o_mine, o_part, hidden_ref, base_ref, *refs):
    sent = refs[: NY - 1]
    joined, pieces = refs[NY - 1 :]
    tokens, width = hidden_ref.shape[1:]
    for source in range(heads_ref.shape[0]):
        for head in range(heads_ref.shape[1] // tokens):
            at = (source * (heads_ref.shape[1] // tokens) + head) * HD
            joined[:, at : at + HD] = heads_ref[source, head * tokens : (head + 1) * tokens, :]
    for half, weight in enumerate((o_mine, o_part)):
        for pair in range(NY // 2):
            at = pair * 2 * width
            product = jnp.dot(
                joined[...], weight[:, at : at + 2 * width], preferred_element_type=jnp.float32
            )
            for inner in range(2):
                step = lax.rem(pair * 2 + inner + NY - y_ref[0], NY)
                pieces[step, half] = product[:, inner * width : (inner + 1) * width]
    base_ref[...] = hidden_ref[...].astype(jnp.float32) + pieces[0]
    for k in range(1, NY):
        sent[k - 1][...] = pieces[k].astype(jnp.bfloat16)


VMEM = pl.BlockSpec(memory_space=pltpu.VMEM)
SMEM = pl.BlockSpec(memory_space=pltpu.SMEM)


def summed_over(value, axis, steps):
    count = lax.axis_size(axis)
    got = [
        lax.ppermute(value, axis, [(i, i ^ step) for i in range(count)]) for step in steps
    ]
    if len(got) == 1:
        return value + got[0]
    return (value + got[0]) + (got[1] + got[2])


def local(inputs, target, norm_gains, w_query, w_keyval, w_output, noise_seed, step_count):
    section = lax.axis_index("section")
    sections = lax.axis_size("section")
    y = lax.axis_index("y")
    z = lax.axis_index("z")
    core = lax.axis_index("core")
    tokens, width = inputs.shape
    full = width * NY * NZ * NC
    query_cols = w_query.shape[3]
    keyval_cols = w_keyval.shape[3]
    block = z * NC + core
    amount = jnp.where(core == 0, perturb_scale, -perturb_scale).astype(jnp.float32)
    spread = NZ * NC * width

    def salt(code):
        return mix_bits(mix_bits(step_count[0] * 40503 + (4 * section + code) * 1000003) ^ noise_seed[0])

    gain_noise = noise_of(jnp.arange(full, dtype=jnp.int32), salt(0))
    gains = (norm_gains[0] + amount * gain_noise).reshape(NY, NZ, NC, width)
    gains = lax.dynamic_index_in_dim(gains, z, 1, keepdims=False)
    gains = jnp.where(core == 0, gains, gains[:, ::-1])
    gains = gains.transpose(1, 0, 2)
    gains = jnp.concatenate([gains, gains], axis=1)[:, ::-1]
    gains = lax.dynamic_slice_in_dim(gains, NY - 1 - y, NY, 1)

    wq, wk, wo = w_query[0, 0], w_keyval[0, 0], w_output[0, 0]
    ints = jnp.stack([salt(1), salt(2), block * width, y * query_cols, y * keyval_cols])
    ints_out = jnp.stack([salt(3), y * query_cols, block * width])
    hidden = jnp.stack([inputs, swapped(inputs)])
    goal = jnp.stack([target, swapped(target)])
    gains, ints, ints_out, gain_noise, hidden, goal = lax.optimization_barrier(
        (gains, ints, ints_out, gain_noise, hidden, goal)
    )
    paired = jax.ShapeDtypeStruct((wq.shape[0], query_cols + keyval_cols), jnp.bfloat16)
    zq, zk, in_mine, in_other = pl.pallas_call(
        functools.partial(perturb_input_kernel, full, spread, NY),
        grid=(NY,),
        in_specs=[SMEM, SMEM, by_rows(wq, NY), by_rows(wk, NY)],
        out_specs=[by_rows(wq, NY), by_rows(wk, NY), by_rows(paired, NY), by_rows(paired, NY)],
        out_shape=[
            pltpu.HBM(wq.shape, jnp.bfloat16),
            pltpu.HBM(wk.shape, jnp.bfloat16),
            paired,
            paired,
        ],
        compiler_params=limit(14),
        cost_estimate=noise_cost(wq.size + wk.size),
    )(
        ints,
        amount.reshape(1), in_hbm(wq), in_hbm(wk),
    )
    in_part = swapped(in_other)
    around = [hidden] + [shifted(hidden, "y", NY, k) for k in range(1, NY)]
    zo, o_mine, o_other = pl.pallas_call(
        functools.partial(perturb_output_kernel, full, spread, width),
        grid=(4,),
        in_specs=[SMEM, SMEM, by_rows(wo, 4)],
        out_specs=[by_rows(wo, 4)] * 3,
        out_shape=[
            pltpu.HBM(wo.shape, jnp.bfloat16),
            jax.ShapeDtypeStruct(wo.shape, jnp.bfloat16),
            jax.ShapeDtypeStruct(wo.shape, jnp.bfloat16),
        ],
        compiler_params=limit(14),
        cost_estimate=noise_cost(wo.size),
    )(
        ints_out,
        amount.reshape(1), in_hbm(wo),
    )
    o_part = swapped(o_other)
    in_mine, in_part, o_mine, o_part = lax.optimization_barrier((in_mine, in_part, o_mine, o_part))

    cosine, sine = (jnp.asarray(t) for t in rope_tables(tokens))
    place = y.reshape(1)
    heads_z = query_cols // HD // NZ
    rows = (heads_z + 2) * tokens + 16

    def project(around):
        return pl.pallas_call(
            project_kernel,
            in_specs=[SMEM] + [VMEM] * (NY + 3),
            out_specs=VMEM,
            out_shape=jax.ShapeDtypeStruct((NZ, rows, HD), jnp.bfloat16),
            scratch_shapes=[pltpu.VMEM((NC, tokens, NY * width), jnp.bfloat16)],
            compiler_params=limit(14),
        )(place, *around, gains, in_mine, in_part)

    def attend(received):
        return pl.pallas_call(
            functools.partial(attend_kernel, full),
            in_specs=[VMEM] * 3,
            out_specs=VMEM,
            out_shape=jax.ShapeDtypeStruct((NZ, heads_z * tokens, HD), jnp.bfloat16),
            compiler_params=limit(14),
        )(received, cosine, sine)

    def output(heads, hidden):
        return pl.pallas_call(
            output_kernel,
            in_specs=[SMEM] + [VMEM] * 4,
            out_specs=[VMEM] * NY,
            out_shape=[jax.ShapeDtypeStruct(hidden.shape, jnp.float32)]
            + [jax.ShapeDtypeStruct(hidden.shape, jnp.bfloat16)] * (NY - 1),
            scratch_shapes=[
                pltpu.VMEM((tokens, query_cols), jnp.bfloat16),
                pltpu.VMEM((NY,) + hidden.shape, jnp.float32),
            ],
            compiler_params=limit(14),
        )(place, heads, o_mine, o_part, hidden)

    record = jnp.zeros_like(hidden)
    for tick in range(4):
        if tick:
            around = [hidden] + [shifted(hidden, "y", NY, k) for k in range(1, NY)]
        received = lax.all_to_all(project(around), "z", 0, 0, tiled=True)
        heads = lax.all_to_all(attend(received), "z", 0, 0, tiled=True)
        base, *pieces = output(heads, hidden)
        pieces = [shifted(piece, "y", NY, k) for k, piece in enumerate(pieces, 1)]
        if tick < 3:
            for piece in pieces:
                base = base + piece.astype(jnp.float32)
            result = base.astype(jnp.bfloat16)
            record = jnp.where(section == tick, result, record)
            hidden = lax.ppermute(result, "section", [(tick, tick + 1)])
        else:
            result, squared = pl.pallas_call(
                finish_kernel,
                in_specs=[VMEM] * (NY + 1),
                out_specs=[VMEM] * 2,
                out_shape=[
                    jax.ShapeDtypeStruct(hidden.shape, jnp.bfloat16),
                    jax.ShapeDtypeStruct((8, LANE), jnp.float32),
                ],
                compiler_params=limit(8),
            )(base, *pieces, goal)
            record = jnp.where(section == tick, result, record)

    squared = summed_over(squared, "y", (1, 2, 3))
    squared = summed_over(squared, "z", (1,))
    squared = summed_over(squared, "z", (2, 4, 6))
    copies = [lax.ppermute(squared, "section", [(sections - 1, k)]) for k in range(sections - 1)]
    squared = jnp.where(section == sections - 1, squared, sum(copies[1:], copies[0]))
    mine, other = record[0], swapped(record[1])
    layer_outputs = jnp.where(core == 0, jnp.stack([mine, other]), jnp.stack([other, mine]))[None]
    squared, layer_outputs = lax.optimization_barrier((squared, layer_outputs))
    partner = swapped(squared)

    arrays = (wq, wk, wo)
    specs = [by_rows(w, 8) for w in arrays]
    tile = pl.BlockSpec((8, LANE), lambda i: (0, 0))
    line = pl.BlockSpec((1, full), lambda i: (0, 0))
    new_query, new_keyval, new_output, losses, new_gains = pl.pallas_call(
        functools.partial(update_kernel, float(tokens * full)),
        grid=(8,),
        in_specs=[SMEM, tile, tile, line, line] + specs + specs,
        out_specs=specs + [SMEM, line],
        out_shape=[pltpu.HBM(w.shape, jnp.bfloat16) for w in arrays]
        + [jax.ShapeDtypeStruct((1, 2), jnp.float32), jax.ShapeDtypeStruct((1, full), jnp.float32)],
        scratch_shapes=[pltpu.SMEM((1,), jnp.float32)],
        compiler_params=limit(14),
    )(core.reshape(1), squared, partner, norm_gains, gain_noise[None], *map(in_hbm, (*arrays, zq, zk, zo)))
    return (
        layer_outputs,
        losses,
        new_gains,
        new_query[None, None],
        new_keyval[None, None],
        new_output[None, None],
    )


def solution(mesh):
    mesh = Mesh(mesh.devices.reshape(-1, NY, NZ, NC), ("section", "y", "z", "core"))
    tensor = ("y", "z", "core")
    return jax.shard_map(
        local,
        mesh=mesh,
        in_specs=(
            P(None, tensor),
            P(None, tensor),
            P("section", None),
            P("section", tensor, None, None),
            P("section", tensor, None, None),
            P("section", tensor, None, None),
            P(),
            P(),
        ),
        out_specs=(
            P("section", None, None, tensor),
            P("section", None),
            P("section", None),
            P("section", tensor, None, None),
            P("section", tensor, None, None),
            P("section", tensor, None, None),
        ),
        check_vma=False,
    )
```

```python
import functools

import jax
import jax.numpy as jnp
import numpy as np
from jax import lax
from jax.experimental import pallas as pl
from jax.experimental.pallas import tpu as pltpu
from jax.sharding import Mesh, PartitionSpec as P

HD = 128
NY, NZ, NC = 4, 8, 2
LANE = 128

perturb_scale = 0.001
learn_rate = 1e-05
rope_base = 500000.0


def logical(value, by):
    return lax.shift_right_logical(value, jnp.full(value.shape, by, value.dtype))


def mix_bits(hashed):
    hashed = hashed ^ logical(hashed, 16)
    hashed = hashed * jnp.int32(2146121005)
    hashed = hashed ^ logical(hashed, 15)
    hashed = hashed * jnp.int32(-2073254261)
    hashed = hashed ^ logical(hashed, 16)
    return hashed


def noise_of(index, salt):
    hashed = mix_bits(mix_bits(index ^ salt) + salt)
    return logical(hashed, 8).astype(jnp.float32) * (3.4641016 / 16777216.0) - 0.5 * 3.4641016


def limit(mib):
    return pltpu.CompilerParams(vmem_limit_bytes=mib * 1024 * 1024)


def perturb_input_kernel(full, spread, groups, ints_ref, sign_ref, q_ref, k_ref, zq_ref, zk_ref, mine_ref, other_ref):
    rows, query_cols = q_ref.shape
    keyval_cols = k_ref.shape[1]
    row = lax.broadcasted_iota(jnp.int32, (rows, 1), 0) + pl.program_id(0) * spread + ints_ref[2]
    for w_ref, z_ref, at, salt, cols, first in (
        (q_ref, zq_ref, 0, ints_ref[0], full, ints_ref[3]),
        (k_ref, zk_ref, query_cols, ints_ref[1], keyval_cols * groups, ints_ref[4]),
    ):
        width = w_ref.shape[1]
        col = lax.broadcasted_iota(jnp.int32, (1, width), 1) + first
        z = noise_of(row * cols + col, salt)
        z_ref[...] = z.astype(jnp.bfloat16)
        w = w_ref[...].astype(jnp.float32)
        shift = sign_ref[0] * z
        mine_ref[:, at : at + width] = (w + shift).astype(jnp.bfloat16)
        other_ref[:, at : at + width] = (w - shift).astype(jnp.bfloat16)


def perturb_output_kernel(full, spread, width, ints_ref, sign_ref, w_ref, z_ref, mine_ref, other_ref):
    rows, cols = w_ref.shape
    row = lax.broadcasted_iota(jnp.int32, (rows, 1), 0) + pl.program_id(0) * rows + ints_ref[1]
    col = lax.broadcasted_iota(jnp.int32, (1, cols), 1)
    col = col + col // width * (spread - width) + ints_ref[2]
    z = noise_of(row * full + col, ints_ref[0])
    z_ref[...] = z.astype(jnp.bfloat16)
    w = w_ref[...].astype(jnp.float32)
    shift = sign_ref[0] * z
    mine_ref[...] = (w + shift).astype(jnp.bfloat16)
    other_ref[...] = (w - shift).astype(jnp.bfloat16)


def sum_kernel(base_ref, *refs):
    pieces, result_ref = refs[:-1], refs[-1]
    for half in range(NC):
        summed = base_ref[half]
        for piece in pieces:
            summed = summed + piece[half].astype(jnp.float32)
        result_ref[half] = summed.astype(jnp.bfloat16)


def finish_kernel(base_ref, *refs):
    goals, result_ref, gap_ref = refs[-4:-2], refs[-2], refs[-1]
    sum_kernel(base_ref, *refs[: NY - 1], result_ref)
    total = jnp.zeros(gap_ref.shape, jnp.float32)
    for half, goal_ref in enumerate(goals):
        gap = result_ref[half].astype(jnp.float32) - goal_ref[...].astype(jnp.float32)
        total = total + jnp.sum((gap * gap).reshape((-1,) + gap_ref.shape), axis=0)
    gap_ref[...] = total


def update_kernel(
    entries, chunks, core_ref, own_ref, partner_ref, gain_ref, noise_ref, mine_ref, other_ref, *refs
):
    stored, noises, outs = refs[:3], refs[3:6], refs[6:9]
    loss_ref, new_gain_ref, layer_ref = refs[9:12]
    held = refs[12:18]
    made = refs[18:21]
    load_sems, store_sems = refs[21:]

    def part(ref, chunk):
        rows = ref.shape[0] // chunks
        return ref.at[pl.ds(chunk * rows, rows)]

    def load(which, chunk):
        source = (stored + noises)[which]
        return pltpu.make_async_copy(
            part(source, chunk), part(held[which], chunk), load_sems.at[which, chunk]
        )

    def store(which, chunk):
        return pltpu.make_async_copy(
            part(made[which], chunk), part(outs[which], chunk), store_sems.at[which, chunk]
        )

    for chunk in range(chunks):
        for which in range(6):
            load(which, chunk).start()
    own = jnp.sum(own_ref[...]) / entries
    partner = jnp.sum(partner_ref[...]) / entries
    first = core_ref[0] == 0
    plus = jnp.where(first, own, partner)
    minus = jnp.where(first, partner, own)
    loss_ref[0, 0] = plus
    loss_ref[0, 1] = minus
    rate = learn_rate * ((plus - minus) / (2.0 * perturb_scale))
    new_gain_ref[...] = gain_ref[...] - rate * noise_ref[...]
    layer_ref[0, core_ref[0]] = mine_ref[...]
    layer_ref[0, 1 - core_ref[0]] = other_ref[...]
    for chunk in range(chunks):
        for which in range(3):
            load(which, chunk).wait()
            load(3 + which, chunk).wait()
            w = part(held[which], chunk)[...].astype(jnp.float32)
            z = part(held[3 + which], chunk)[...].astype(jnp.float32)
            part(made[which], chunk)[...] = (w - rate * z).astype(jnp.bfloat16)
            store(which, chunk).start()
    for chunk in range(chunks):
        for which in range(3):
            store(which, chunk).wait()


def in_hbm(array):
    return pltpu.with_memory_space_constraint(array, pltpu.HBM)


def by_rows(array, steps):
    return pl.BlockSpec((array.shape[0] // steps, array.shape[1]), lambda i: (i, 0))


def noise_cost(count):
    return pl.CostEstimate(flops=60 * count, bytes_accessed=10 * count, transcendentals=0)


def shifted(array, axis, count, by):
    return lax.ppermute(array, axis, [(i, (i + by) % count) for i in range(count)])


def swapped(array):
    return lax.ppermute(array, "core", [(0, 1), (1, 0)])


def rope_tables(tokens):
    half = HD // 2
    frequency = np.float32(rope_base) ** (-np.arange(half, dtype=np.float32) * np.float32(2.0) / np.float32(HD))
    angles = np.arange(tokens, dtype=np.float32)[:, None] * frequency.astype(np.float32)[None, :]
    cosine = np.cos(angles.astype(np.float64)).astype(np.float32)
    sine = np.sin(angles.astype(np.float64)).astype(np.float32)
    return np.concatenate([cosine, cosine], 1), np.concatenate([-sine, sine], 1)


def rotate(values, cosine, sine):
    return values * cosine + pltpu.roll(values, HD // 2, 1) * sine


def same_index(size):
    return lax.broadcasted_iota(jnp.int32, (size, size), 0) == lax.broadcasted_iota(
        jnp.int32, (size, size), 1
    )


def project_kernel(y_ref, *refs):
    around = refs[:NY]
    gains_ref, mine, part, out_ref, scaled = refs[NY:]
    tokens, width = around[0].shape[1:]
    total = jnp.zeros((tokens, 1), jnp.float32)
    for k in range(NY):
        place = pl.multiple_of(lax.rem(y_ref[0] + (NY - k), NY) * width, width)
        for half in range(NC):
            wide = around[k][half].astype(jnp.float32)
            total = total + jnp.sum(wide * wide, axis=1, keepdims=True)
            scaled[half, :, pl.ds(place, width)] = (wide * gains_ref[half, k : k + 1, :]).astype(jnp.bfloat16)

    def product(start, size):
        return jnp.dot(
            scaled[0], mine[:, start : start + size], preferred_element_type=jnp.float32
        ) + jnp.dot(scaled[1], part[:, start : start + size], preferred_element_type=jnp.float32)

    kept = out_ref.shape[1] - 16 - 2 * tokens
    span = kept // tokens * HD
    for dest in range(NZ):
        query = product(dest * span, span).astype(jnp.bfloat16)
        for head in range(span // HD):
            out_ref[dest, head * tokens : (head + 1) * tokens, :] = query[:, head * HD : (head + 1) * HD]
    groups = (mine.shape[1] - NZ * span) // (2 * HD)
    for group in range(groups):
        keyval = product(NZ * span + group * 2 * HD, 2 * HD).astype(jnp.bfloat16)
        for dest in range(group * NZ // groups, (group + 1) * NZ // groups):
            out_ref[dest, kept : kept + tokens, :] = keyval[:, :HD]
            out_ref[dest, kept + tokens : kept + 2 * tokens, :] = keyval[:, HD:]
    row = jnp.sum(jnp.where(same_index(tokens), total, 0.0), axis=0, keepdims=True)
    high = row.astype(jnp.bfloat16).astype(jnp.float32)
    line = lax.broadcasted_iota(jnp.int32, (16, tokens), 0)
    extra = jnp.where(line == 0, high, jnp.where(line == 1, row - high, 0.0)).astype(jnp.bfloat16)
    for dest in range(NZ):
        out_ref[dest, kept + 2 * tokens :, :] = extra


def attend_kernel(full, recv_ref, cos_ref, sin_ref, out_ref):
    tokens = cos_ref.shape[0]
    heads = out_ref.shape[1] // tokens

    def total(start, size):
        acc = recv_ref[0, start : start + size, :].astype(jnp.float32)
        for source in range(1, NZ):
            acc = acc + recv_ref[source, start : start + size, :].astype(jnp.float32)
        return acc

    cosine = cos_ref[...]
    sine = sin_ref[...]
    kept = heads * tokens
    squares = total(kept + 2 * tokens, 16)
    row = squares[0:1] + squares[1:2]
    column = jnp.sum(jnp.where(same_index(tokens), row, 0.0), axis=1, keepdims=True)
    inverse = lax.rsqrt(column / full + 1e-05)
    key = (total(kept, tokens) * inverse).astype(jnp.bfloat16).astype(jnp.float32)
    key = rotate(key, cosine, sine)
    value = (total(kept + tokens, tokens) * inverse).astype(jnp.bfloat16)
    causal = lax.broadcasted_iota(jnp.int32, (tokens, tokens), 0) >= lax.broadcasted_iota(
        jnp.int32, (tokens, tokens), 1
    )
    for head in range(heads):
        query = rotate(total(head * tokens, tokens) * inverse, cosine, sine)
        scores = lax.dot_general(
            query, key, (((1,), (1,)), ((), ())),
            precision=lax.Precision.HIGHEST, preferred_element_type=jnp.float32,
        ) * (1.0 / np.sqrt(np.float32(HD)))
        expo = jnp.where(causal, jnp.exp(scores), 0.0)
        weights = (expo / jnp.sum(expo, axis=1, keepdims=True)).astype(jnp.bfloat16)
        mixed = jnp.dot(weights, value, preferred_element_type=jnp.float32).astype(jnp.bfloat16)
        for dest in range(NZ):
            out_ref[dest, head * tokens : (head + 1) * tokens, :] = mixed


def output_kernel(y_ref, heads_ref, o_mine, o_part, hidden_ref, base_ref, *refs):
    sent = refs[: NY - 1]
    joined, pieces = refs[NY - 1 :]
    tokens, width = hidden_ref.shape[1:]
    for source in range(heads_ref.shape[0]):
        for head in range(heads_ref.shape[1] // tokens):
            at = (source * (heads_ref.shape[1] // tokens) + head) * HD
            joined[:, at : at + HD] = heads_ref[source, head * tokens : (head + 1) * tokens, :]
    for half, weight in enumerate((o_mine, o_part)):
        for pair in range(NY // 2):
            at = pair * 2 * width
            product = jnp.dot(
                joined[...], weight[:, at : at + 2 * width], preferred_element_type=jnp.float32
            )
            for inner in range(2):
                step = lax.rem(pair * 2 + inner + NY - y_ref[0], NY)
                pieces[step, half] = product[:, inner * width : (inner + 1) * width]
    base_ref[...] = hidden_ref[...].astype(jnp.float32) + pieces[0]
    for k in range(1, NY):
        sent[k - 1][...] = pieces[k].astype(jnp.bfloat16)


VMEM = pl.BlockSpec(memory_space=pltpu.VMEM)
SMEM = pl.BlockSpec(memory_space=pltpu.SMEM)


def summed_over(value, axis, steps):
    count = lax.axis_size(axis)
    got = [
        lax.ppermute(value, axis, [(i, i ^ step) for i in range(count)]) for step in steps
    ]
    if len(got) == 1:
        return value + got[0]
    return (value + got[0]) + (got[1] + got[2])


def local(inputs, target, norm_gains, w_query, w_keyval, w_output, noise_seed, step_count):
    section = lax.axis_index("section")
    sections = lax.axis_size("section")
    y = lax.axis_index("y")
    z = lax.axis_index("z")
    core = lax.axis_index("core")
    tokens, width = inputs.shape
    full = width * NY * NZ * NC
    query_cols = w_query.shape[3]
    keyval_cols = w_keyval.shape[3]
    block = z * NC + core
    amount = jnp.where(core == 0, perturb_scale, -perturb_scale).astype(jnp.float32)
    spread = NZ * NC * width

    def salt(code):
        return mix_bits(mix_bits(step_count[0] * 40503 + (4 * section + code) * 1000003) ^ noise_seed[0])

    gain_noise = noise_of(jnp.arange(full, dtype=jnp.int32), salt(0))
    gains = (norm_gains[0] + amount * gain_noise).reshape(NY, NZ, NC, width)
    gains = lax.dynamic_index_in_dim(gains, z, 1, keepdims=False)
    gains = jnp.where(core == 0, gains, gains[:, ::-1])
    gains = gains.transpose(1, 0, 2)
    gains = jnp.concatenate([gains, gains], axis=1)[:, ::-1]
    gains = lax.dynamic_slice_in_dim(gains, NY - 1 - y, NY, 1)

    wq, wk, wo = w_query[0, 0], w_keyval[0, 0], w_output[0, 0]
    ints = jnp.stack([salt(1), salt(2), block * width, y * query_cols, y * keyval_cols])
    ints_out = jnp.stack([salt(3), y * query_cols, block * width])
    hidden = jnp.stack([inputs, swapped(inputs)])
    target_part = swapped(target)
    gains, ints, ints_out, gain_noise, hidden, target_part = lax.optimization_barrier(
        (gains, ints, ints_out, gain_noise, hidden, target_part)
    )
    paired = jax.ShapeDtypeStruct((wq.shape[0], query_cols + keyval_cols), jnp.bfloat16)
    zq, zk, in_mine, in_other = pl.pallas_call(
        functools.partial(perturb_input_kernel, full, spread, NY),
        grid=(NY,),
        in_specs=[SMEM, SMEM, by_rows(wq, NY), by_rows(wk, NY)],
        out_specs=[by_rows(wq, NY), by_rows(wk, NY), by_rows(paired, NY), by_rows(paired, NY)],
        out_shape=[
            pltpu.HBM(wq.shape, jnp.bfloat16),
            pltpu.HBM(wk.shape, jnp.bfloat16),
            paired,
            paired,
        ],
        compiler_params=limit(14),
        cost_estimate=noise_cost(wq.size + wk.size),
    )(
        ints,
        amount.reshape(1), in_hbm(wq), in_hbm(wk),
    )
    in_part = swapped(in_other)
    around = [hidden] + [shifted(hidden, "y", NY, k) for k in range(1, NY)]
    zo, o_mine, o_other = pl.pallas_call(
        functools.partial(perturb_output_kernel, full, spread, width),
        grid=(4,),
        in_specs=[SMEM, SMEM, by_rows(wo, 4)],
        out_specs=[by_rows(wo, 4)] * 3,
        out_shape=[
            pltpu.HBM(wo.shape, jnp.bfloat16),
            jax.ShapeDtypeStruct(wo.shape, jnp.bfloat16),
            jax.ShapeDtypeStruct(wo.shape, jnp.bfloat16),
        ],
        compiler_params=limit(14),
        cost_estimate=noise_cost(wo.size),
    )(
        ints_out,
        amount.reshape(1), in_hbm(wo),
    )
    o_part = swapped(o_other)
    in_mine, in_part, o_mine, o_part = lax.optimization_barrier((in_mine, in_part, o_mine, o_part))

    cosine, sine = (jnp.asarray(t) for t in rope_tables(tokens))
    place = y.reshape(1)
    heads_z = query_cols // HD // NZ
    rows = (heads_z + 2) * tokens + 16

    def project(around):
        return pl.pallas_call(
            project_kernel,
            in_specs=[SMEM] + [VMEM] * (NY + 3),
            out_specs=VMEM,
            out_shape=jax.ShapeDtypeStruct((NZ, rows, HD), jnp.bfloat16),
            scratch_shapes=[pltpu.VMEM((NC, tokens, NY * width), jnp.bfloat16)],
            compiler_params=limit(14),
        )(place, *around, gains, in_mine, in_part)

    def attend(received):
        return pl.pallas_call(
            functools.partial(attend_kernel, full),
            in_specs=[VMEM] * 3,
            out_specs=VMEM,
            out_shape=jax.ShapeDtypeStruct((NZ, heads_z * tokens, HD), jnp.bfloat16),
            compiler_params=limit(14),
        )(received, cosine, sine)

    def output(heads, hidden):
        return pl.pallas_call(
            output_kernel,
            in_specs=[SMEM] + [VMEM] * 4,
            out_specs=[VMEM] * NY,
            out_shape=[jax.ShapeDtypeStruct(hidden.shape, jnp.float32)]
            + [jax.ShapeDtypeStruct(hidden.shape, jnp.bfloat16)] * (NY - 1),
            scratch_shapes=[
                pltpu.VMEM((tokens, query_cols), jnp.bfloat16),
                pltpu.VMEM((NY,) + hidden.shape, jnp.float32),
            ],
            compiler_params=limit(14),
        )(place, heads, o_mine, o_part, hidden)

    record = jnp.zeros_like(hidden)
    for tick in range(4):
        if tick:
            around = [hidden] + [shifted(hidden, "y", NY, k) for k in range(1, NY)]
        received = lax.all_to_all(project(around), "z", 0, 0, tiled=True)
        heads = lax.all_to_all(attend(received), "z", 0, 0, tiled=True)
        base, *pieces = output(heads, hidden)
        pieces = [shifted(piece, "y", NY, k) for k, piece in enumerate(pieces, 1)]
        if tick < 3:
            result = pl.pallas_call(
                sum_kernel,
                in_specs=[VMEM] * NY,
                out_specs=VMEM,
                out_shape=jax.ShapeDtypeStruct(hidden.shape, jnp.bfloat16),
                compiler_params=limit(8),
            )(base, *pieces)
            record = jnp.where(section == tick, result, record)
            hidden = lax.ppermute(result, "section", [(tick, tick + 1)])
        else:
            result, squared = pl.pallas_call(
                finish_kernel,
                in_specs=[VMEM] * (NY + 2),
                out_specs=[VMEM] * 2,
                out_shape=[
                    jax.ShapeDtypeStruct(hidden.shape, jnp.bfloat16),
                    jax.ShapeDtypeStruct((8, LANE), jnp.float32),
                ],
                compiler_params=limit(8),
            )(base, *pieces, target, target_part)
            record = jnp.where(section == tick, result, record)

    squared = summed_over(squared, "y", (1, 2, 3))
    squared = summed_over(squared, "z", (1,))
    squared = summed_over(squared, "z", (2, 4, 6))
    copies = [lax.ppermute(squared, "section", [(sections - 1, k)]) for k in range(sections - 1)]
    squared = jnp.where(section == sections - 1, squared, sum(copies[1:], copies[0]))
    mine, other = record[0], swapped(record[1])
    partner = swapped(squared)

    arrays = (wq, wk, wo)
    chunks = 4
    far = pl.BlockSpec(memory_space=pl.ANY)
    new_query, new_keyval, new_output, losses, new_gains, layer_outputs = pl.pallas_call(
        functools.partial(update_kernel, float(tokens * full), chunks),
        in_specs=[SMEM] + [VMEM] * 6 + [far] * 6,
        out_specs=[far] * 3 + [SMEM] + [VMEM] * 2,
        out_shape=[pltpu.HBM(w.shape, jnp.bfloat16) for w in arrays]
        + [
            jax.ShapeDtypeStruct((1, 2), jnp.float32),
            jax.ShapeDtypeStruct((1, full), jnp.float32),
            jax.ShapeDtypeStruct((1, 2) + mine.shape, jnp.bfloat16),
        ],
        scratch_shapes=[pltpu.VMEM(w.shape, jnp.bfloat16) for w in arrays * 3]
        + [pltpu.SemaphoreType.DMA((6, chunks)), pltpu.SemaphoreType.DMA((3, chunks))],
        compiler_params=limit(24),
    )(
        core.reshape(1), squared, partner, norm_gains, gain_noise[None], mine, other,
        *map(in_hbm, (*arrays, zq, zk, zo)),
    )
    return (
        layer_outputs,
        losses,
        new_gains,
        new_query[None, None],
        new_keyval[None, None],
        new_output[None, None],
    )


def solution(mesh):
    mesh = Mesh(mesh.devices.reshape(-1, NY, NZ, NC), ("section", "y", "z", "core"))
    tensor = ("y", "z", "core")
    return jax.shard_map(
        local,
        mesh=mesh,
        in_specs=(
            P(None, tensor),
            P(None, tensor),
            P("section", None),
            P("section", tensor, None, None),
            P("section", tensor, None, None),
            P("section", tensor, None, None),
            P(),
            P(),
        ),
        out_specs=(
            P("section", None, None, tensor),
            P("section", None),
            P("section", None),
            P("section", tensor, None, None),
            P("section", tensor, None, None),
            P("section", tensor, None, None),
        ),
        check_vma=False,
    )
```

```python
import functools

import jax
import jax.numpy as jnp
import numpy as np
from jax import lax
from jax.experimental import pallas as pl
from jax.experimental.pallas import tpu as pltpu
from jax.sharding import Mesh, PartitionSpec as P

HD = 128
NY, NZ, NC = 4, 8, 2
LANE = 128

perturb_scale = 0.001
learn_rate = 1e-05
rope_base = 500000.0


def logical(value, by):
    return lax.shift_right_logical(value, jnp.full(value.shape, by, value.dtype))


def mix_bits(hashed):
    hashed = hashed ^ logical(hashed, 16)
    hashed = hashed * jnp.int32(2146121005)
    hashed = hashed ^ logical(hashed, 15)
    hashed = hashed * jnp.int32(-2073254261)
    hashed = hashed ^ logical(hashed, 16)
    return hashed


def noise_of(index, salt):
    hashed = mix_bits(mix_bits(index ^ salt) + salt)
    return logical(hashed, 8).astype(jnp.float32) * (3.4641016 / 16777216.0) - 0.5 * 3.4641016


def limit(mib):
    return pltpu.CompilerParams(vmem_limit_bytes=mib * 1024 * 1024)


def perturb_input_kernel(full, spread, groups, ints_ref, sign_ref, q_ref, k_ref, zq_ref, zk_ref, mine_ref, other_ref):
    rows, query_cols = q_ref.shape
    keyval_cols = k_ref.shape[1]
    row = lax.broadcasted_iota(jnp.int32, (rows, 1), 0) + pl.program_id(0) * spread + ints_ref[2]
    for w_ref, z_ref, at, salt, cols, first in (
        (q_ref, zq_ref, 0, ints_ref[0], full, ints_ref[3]),
        (k_ref, zk_ref, query_cols, ints_ref[1], keyval_cols * groups, ints_ref[4]),
    ):
        width = w_ref.shape[1]
        col = lax.broadcasted_iota(jnp.int32, (1, width), 1) + first
        z = noise_of(row * cols + col, salt)
        z_ref[...] = z.astype(jnp.bfloat16)
        w = w_ref[...].astype(jnp.float32)
        shift = sign_ref[0] * z
        mine_ref[:, at : at + width] = (w + shift).astype(jnp.bfloat16)
        other_ref[:, at : at + width] = (w - shift).astype(jnp.bfloat16)


def perturb_output_kernel(full, spread, width, ints_ref, sign_ref, w_ref, z_ref, mine_ref, other_ref):
    rows, cols = w_ref.shape
    row = lax.broadcasted_iota(jnp.int32, (rows, 1), 0) + pl.program_id(0) * rows + ints_ref[1]
    col = lax.broadcasted_iota(jnp.int32, (1, cols), 1)
    col = col + col // width * (spread - width) + ints_ref[2]
    z = noise_of(row * full + col, ints_ref[0])
    z_ref[...] = z.astype(jnp.bfloat16)
    w = w_ref[...].astype(jnp.float32)
    shift = sign_ref[0] * z
    mine_ref[...] = (w + shift).astype(jnp.bfloat16)
    other_ref[...] = (w - shift).astype(jnp.bfloat16)


def sum_kernel(base_ref, *refs):
    pieces, result_ref = refs[:-1], refs[-1]
    for half in range(NC):
        summed = base_ref[half]
        for piece in pieces:
            summed = summed + piece[half].astype(jnp.float32)
        result_ref[half] = summed.astype(jnp.bfloat16)


def finish_kernel(base_ref, *refs):
    goals, result_ref, gap_ref = refs[-4:-2], refs[-2], refs[-1]
    sum_kernel(base_ref, *refs[: NY - 1], result_ref)
    total = jnp.zeros(gap_ref.shape, jnp.float32)
    for half, goal_ref in enumerate(goals):
        gap = result_ref[half].astype(jnp.float32) - goal_ref[...].astype(jnp.float32)
        total = total + jnp.sum((gap * gap).reshape((-1,) + gap_ref.shape), axis=0)
    gap_ref[...] = total


def fetch_kernel(*refs):
    sems = refs[-1]
    count = len(refs) // 2
    copies = [
        pltpu.make_async_copy(refs[i], refs[count + i], sems.at[i]) for i in range(count)
    ]
    for copy in copies:
        copy.start()
    for copy in copies:
        copy.wait()


def update_kernel(
    entries, chunks, core_ref, own_ref, partner_ref, gain_ref, noise_ref, mine_ref, other_ref, *refs
):
    held, outs = refs[:6], refs[6:9]
    loss_ref, new_gain_ref, layer_ref = refs[9:12]
    made = refs[12:15]
    store_sems = refs[15]

    def part(ref, chunk):
        rows = ref.shape[0] // chunks
        return ref.at[pl.ds(chunk * rows, rows)]

    def store(which, chunk):
        return pltpu.make_async_copy(
            part(made[which], chunk), part(outs[which], chunk), store_sems.at[which, chunk]
        )

    own = jnp.sum(own_ref[...]) / entries
    partner = jnp.sum(partner_ref[...]) / entries
    first = core_ref[0] == 0
    plus = jnp.where(first, own, partner)
    minus = jnp.where(first, partner, own)
    loss_ref[0, 0] = plus
    loss_ref[0, 1] = minus
    rate = learn_rate * ((plus - minus) / (2.0 * perturb_scale))
    for chunk in range(chunks):
        for which in range(3):
            w = part(held[which], chunk)[...].astype(jnp.float32)
            z = part(held[3 + which], chunk)[...].astype(jnp.float32)
            part(made[which], chunk)[...] = (w - rate * z).astype(jnp.bfloat16)
            store(which, chunk).start()
    new_gain_ref[...] = gain_ref[...] - rate * noise_ref[...]
    layer_ref[0, core_ref[0]] = mine_ref[...]
    layer_ref[0, 1 - core_ref[0]] = other_ref[...]
    for chunk in range(chunks):
        for which in range(3):
            store(which, chunk).wait()


def in_hbm(array):
    return pltpu.with_memory_space_constraint(array, pltpu.HBM)


def by_rows(array, steps):
    return pl.BlockSpec((array.shape[0] // steps, array.shape[1]), lambda i: (i, 0))


def noise_cost(count):
    return pl.CostEstimate(flops=60 * count, bytes_accessed=10 * count, transcendentals=0)


def shifted(array, axis, count, by):
    return lax.ppermute(array, axis, [(i, (i + by) % count) for i in range(count)])


def swapped(array):
    return lax.ppermute(array, "core", [(0, 1), (1, 0)])


def rope_tables(tokens):
    half = HD // 2
    frequency = np.float32(rope_base) ** (-np.arange(half, dtype=np.float32) * np.float32(2.0) / np.float32(HD))
    angles = np.arange(tokens, dtype=np.float32)[:, None] * frequency.astype(np.float32)[None, :]
    cosine = np.cos(angles.astype(np.float64)).astype(np.float32)
    sine = np.sin(angles.astype(np.float64)).astype(np.float32)
    return np.concatenate([cosine, cosine], 1), np.concatenate([-sine, sine], 1)


def rotate(values, cosine, sine):
    return values * cosine + pltpu.roll(values, HD // 2, 1) * sine


def same_index(size):
    return lax.broadcasted_iota(jnp.int32, (size, size), 0) == lax.broadcasted_iota(
        jnp.int32, (size, size), 1
    )


def project_kernel(y_ref, *refs):
    around = refs[:NY]
    gains_ref, mine, part, out_ref, scaled = refs[NY:]
    tokens, width = around[0].shape[1:]
    total = jnp.zeros((tokens, 1), jnp.float32)
    for k in range(NY):
        place = pl.multiple_of(lax.rem(y_ref[0] + (NY - k), NY) * width, width)
        for half in range(NC):
            wide = around[k][half].astype(jnp.float32)
            total = total + jnp.sum(wide * wide, axis=1, keepdims=True)
            scaled[half, :, pl.ds(place, width)] = (wide * gains_ref[half, k : k + 1, :]).astype(jnp.bfloat16)

    def product(start, size):
        return jnp.dot(
            scaled[0], mine[:, start : start + size], preferred_element_type=jnp.float32
        ) + jnp.dot(scaled[1], part[:, start : start + size], preferred_element_type=jnp.float32)

    kept = out_ref.shape[1] - 16 - 2 * tokens
    span = kept // tokens * HD
    for dest in range(NZ):
        query = product(dest * span, span).astype(jnp.bfloat16)
        for head in range(span // HD):
            out_ref[dest, head * tokens : (head + 1) * tokens, :] = query[:, head * HD : (head + 1) * HD]
    groups = (mine.shape[1] - NZ * span) // (2 * HD)
    for group in range(groups):
        keyval = product(NZ * span + group * 2 * HD, 2 * HD).astype(jnp.bfloat16)
        for dest in range(group * NZ // groups, (group + 1) * NZ // groups):
            out_ref[dest, kept : kept + tokens, :] = keyval[:, :HD]
            out_ref[dest, kept + tokens : kept + 2 * tokens, :] = keyval[:, HD:]
    row = jnp.sum(jnp.where(same_index(tokens), total, 0.0), axis=0, keepdims=True)
    high = row.astype(jnp.bfloat16).astype(jnp.float32)
    line = lax.broadcasted_iota(jnp.int32, (16, tokens), 0)
    extra = jnp.where(line == 0, high, jnp.where(line == 1, row - high, 0.0)).astype(jnp.bfloat16)
    for dest in range(NZ):
        out_ref[dest, kept + 2 * tokens :, :] = extra


def attend_kernel(full, recv_ref, cos_ref, sin_ref, out_ref):
    tokens = cos_ref.shape[0]
    heads = out_ref.shape[1] // tokens

    def total(start, size):
        acc = recv_ref[0, start : start + size, :].astype(jnp.float32)
        for source in range(1, NZ):
            acc = acc + recv_ref[source, start : start + size, :].astype(jnp.float32)
        return acc

    cosine = cos_ref[...]
    sine = sin_ref[...]
    kept = heads * tokens
    squares = total(kept + 2 * tokens, 16)
    row = squares[0:1] + squares[1:2]
    column = jnp.sum(jnp.where(same_index(tokens), row, 0.0), axis=1, keepdims=True)
    inverse = lax.rsqrt(column / full + 1e-05)
    key = (total(kept, tokens) * inverse).astype(jnp.bfloat16).astype(jnp.float32)
    key = rotate(key, cosine, sine)
    value = (total(kept + tokens, tokens) * inverse).astype(jnp.bfloat16)
    causal = lax.broadcasted_iota(jnp.int32, (tokens, tokens), 0) >= lax.broadcasted_iota(
        jnp.int32, (tokens, tokens), 1
    )
    for head in range(heads):
        query = rotate(total(head * tokens, tokens) * inverse, cosine, sine)
        scores = lax.dot_general(
            query, key, (((1,), (1,)), ((), ())),
            precision=lax.Precision.HIGHEST, preferred_element_type=jnp.float32,
        ) * (1.0 / np.sqrt(np.float32(HD)))
        expo = jnp.where(causal, jnp.exp(scores), 0.0)
        weights = (expo / jnp.sum(expo, axis=1, keepdims=True)).astype(jnp.bfloat16)
        mixed = jnp.dot(weights, value, preferred_element_type=jnp.float32).astype(jnp.bfloat16)
        for dest in range(NZ):
            out_ref[dest, head * tokens : (head + 1) * tokens, :] = mixed


def output_kernel(y_ref, heads_ref, o_mine, o_part, hidden_ref, base_ref, *refs):
    sent = refs[: NY - 1]
    joined, pieces = refs[NY - 1 :]
    tokens, width = hidden_ref.shape[1:]
    for source in range(heads_ref.shape[0]):
        for head in range(heads_ref.shape[1] // tokens):
            at = (source * (heads_ref.shape[1] // tokens) + head) * HD
            joined[:, at : at + HD] = heads_ref[source, head * tokens : (head + 1) * tokens, :]
    for half, weight in enumerate((o_mine, o_part)):
        for pair in range(NY // 2):
            at = pair * 2 * width
            product = jnp.dot(
                joined[...], weight[:, at : at + 2 * width], preferred_element_type=jnp.float32
            )
            for inner in range(2):
                step = lax.rem(pair * 2 + inner + NY - y_ref[0], NY)
                pieces[step, half] = product[:, inner * width : (inner + 1) * width]
    base_ref[...] = hidden_ref[...].astype(jnp.float32) + pieces[0]
    for k in range(1, NY):
        sent[k - 1][...] = pieces[k].astype(jnp.bfloat16)


VMEM = pl.BlockSpec(memory_space=pltpu.VMEM)
SMEM = pl.BlockSpec(memory_space=pltpu.SMEM)


def summed_over(value, axis, steps):
    count = lax.axis_size(axis)
    got = [
        lax.ppermute(value, axis, [(i, i ^ step) for i in range(count)]) for step in steps
    ]
    if len(got) == 1:
        return value + got[0]
    return (value + got[0]) + (got[1] + got[2])


def local(inputs, target, norm_gains, w_query, w_keyval, w_output, noise_seed, step_count):
    section = lax.axis_index("section")
    sections = lax.axis_size("section")
    y = lax.axis_index("y")
    z = lax.axis_index("z")
    core = lax.axis_index("core")
    tokens, width = inputs.shape
    full = width * NY * NZ * NC
    query_cols = w_query.shape[3]
    keyval_cols = w_keyval.shape[3]
    block = z * NC + core
    amount = jnp.where(core == 0, perturb_scale, -perturb_scale).astype(jnp.float32)
    spread = NZ * NC * width

    def salt(code):
        return mix_bits(mix_bits(step_count[0] * 40503 + (4 * section + code) * 1000003) ^ noise_seed[0])

    gain_noise = noise_of(jnp.arange(full, dtype=jnp.int32), salt(0))
    gains = (norm_gains[0] + amount * gain_noise).reshape(NY, NZ, NC, width)
    gains = lax.dynamic_index_in_dim(gains, z, 1, keepdims=False)
    gains = jnp.where(core == 0, gains, gains[:, ::-1])
    gains = gains.transpose(1, 0, 2)
    gains = jnp.concatenate([gains, gains], axis=1)[:, ::-1]
    gains = lax.dynamic_slice_in_dim(gains, NY - 1 - y, NY, 1)

    wq, wk, wo = w_query[0, 0], w_keyval[0, 0], w_output[0, 0]
    ints = jnp.stack([salt(1), salt(2), block * width, y * query_cols, y * keyval_cols])
    ints_out = jnp.stack([salt(3), y * query_cols, block * width])
    hidden = jnp.stack([inputs, swapped(inputs)])
    target_part = swapped(target)
    gains, ints, ints_out, gain_noise, hidden, target_part = lax.optimization_barrier(
        (gains, ints, ints_out, gain_noise, hidden, target_part)
    )
    paired = jax.ShapeDtypeStruct((wq.shape[0], query_cols + keyval_cols), jnp.bfloat16)
    zq, zk, in_mine, in_other = pl.pallas_call(
        functools.partial(perturb_input_kernel, full, spread, NY),
        grid=(NY,),
        in_specs=[SMEM, SMEM, by_rows(wq, NY), by_rows(wk, NY)],
        out_specs=[by_rows(wq, NY), by_rows(wk, NY), by_rows(paired, NY), by_rows(paired, NY)],
        out_shape=[
            pltpu.HBM(wq.shape, jnp.bfloat16),
            pltpu.HBM(wk.shape, jnp.bfloat16),
            paired,
            paired,
        ],
        compiler_params=limit(14),
        cost_estimate=noise_cost(wq.size + wk.size),
    )(
        ints,
        amount.reshape(1), in_hbm(wq), in_hbm(wk),
    )
    in_part = swapped(in_other)
    around = [hidden] + [shifted(hidden, "y", NY, k) for k in range(1, NY)]
    zo, o_mine, o_other = pl.pallas_call(
        functools.partial(perturb_output_kernel, full, spread, width),
        grid=(4,),
        in_specs=[SMEM, SMEM, by_rows(wo, 4)],
        out_specs=[by_rows(wo, 4)] * 3,
        out_shape=[
            pltpu.HBM(wo.shape, jnp.bfloat16),
            jax.ShapeDtypeStruct(wo.shape, jnp.bfloat16),
            jax.ShapeDtypeStruct(wo.shape, jnp.bfloat16),
        ],
        compiler_params=limit(14),
        cost_estimate=noise_cost(wo.size),
    )(
        ints_out,
        amount.reshape(1), in_hbm(wo),
    )
    o_part = swapped(o_other)
    in_mine, in_part, o_mine, o_part = lax.optimization_barrier((in_mine, in_part, o_mine, o_part))

    cosine, sine = (jnp.asarray(t) for t in rope_tables(tokens))
    place = y.reshape(1)
    heads_z = query_cols // HD // NZ
    rows = (heads_z + 2) * tokens + 16

    def project(around):
        return pl.pallas_call(
            project_kernel,
            in_specs=[SMEM] + [VMEM] * (NY + 3),
            out_specs=VMEM,
            out_shape=jax.ShapeDtypeStruct((NZ, rows, HD), jnp.bfloat16),
            scratch_shapes=[pltpu.VMEM((NC, tokens, NY * width), jnp.bfloat16)],
            compiler_params=limit(14),
        )(place, *around, gains, in_mine, in_part)

    def attend(received):
        return pl.pallas_call(
            functools.partial(attend_kernel, full),
            in_specs=[VMEM] * 3,
            out_specs=VMEM,
            out_shape=jax.ShapeDtypeStruct((NZ, heads_z * tokens, HD), jnp.bfloat16),
            compiler_params=limit(14),
        )(received, cosine, sine)

    def output(heads, hidden):
        return pl.pallas_call(
            output_kernel,
            in_specs=[SMEM] + [VMEM] * 4,
            out_specs=[VMEM] * NY,
            out_shape=[jax.ShapeDtypeStruct(hidden.shape, jnp.float32)]
            + [jax.ShapeDtypeStruct(hidden.shape, jnp.bfloat16)] * (NY - 1),
            scratch_shapes=[
                pltpu.VMEM((tokens, query_cols), jnp.bfloat16),
                pltpu.VMEM((NY,) + hidden.shape, jnp.float32),
            ],
            compiler_params=limit(14),
        )(place, heads, o_mine, o_part, hidden)

    record = jnp.zeros_like(hidden)
    for tick in range(4):
        if tick:
            around = [hidden] + [shifted(hidden, "y", NY, k) for k in range(1, NY)]
        received = lax.all_to_all(project(around), "z", 0, 0, tiled=True)
        heads = lax.all_to_all(attend(received), "z", 0, 0, tiled=True)
        base, *pieces = output(heads, hidden)
        pieces = [shifted(piece, "y", NY, k) for k, piece in enumerate(pieces, 1)]
        if tick < 3:
            result = pl.pallas_call(
                sum_kernel,
                in_specs=[VMEM] * NY,
                out_specs=VMEM,
                out_shape=jax.ShapeDtypeStruct(hidden.shape, jnp.bfloat16),
                compiler_params=limit(8),
            )(base, *pieces)
            record = jnp.where(section == tick, result, record)
            hidden = lax.ppermute(result, "section", [(tick, tick + 1)])
        else:
            result, squared = pl.pallas_call(
                finish_kernel,
                in_specs=[VMEM] * (NY + 2),
                out_specs=[VMEM] * 2,
                out_shape=[
                    jax.ShapeDtypeStruct(hidden.shape, jnp.bfloat16),
                    jax.ShapeDtypeStruct((8, LANE), jnp.float32),
                ],
                compiler_params=limit(8),
            )(base, *pieces, target, target_part)
            record = jnp.where(section == tick, result, record)

    squared = summed_over(squared, "y", (1, 2, 3))
    squared = summed_over(squared, "z", (1,))
    squared = summed_over(squared, "z", (2, 4, 6))
    arrays = (wq, wk, wo, zq, zk, zo)
    squared, *arrays = lax.optimization_barrier((squared, *arrays))
    far = pl.BlockSpec(memory_space=pl.ANY)
    held = pl.pallas_call(
        fetch_kernel,
        in_specs=[far] * 6,
        out_specs=[VMEM] * 6,
        out_shape=[pltpu.VMEM(w.shape, jnp.bfloat16) for w in arrays],
        scratch_shapes=[pltpu.SemaphoreType.DMA((6,))],
        compiler_params=limit(14),
        cost_estimate=pl.CostEstimate(
            flops=0, bytes_accessed=8 * sum(w.size for w in arrays[:3]), transcendentals=0
        ),
    )(*map(in_hbm, arrays))
    copies = [lax.ppermute(squared, "section", [(sections - 1, k)]) for k in range(sections - 1)]
    squared = jnp.where(section == sections - 1, squared, sum(copies[1:], copies[0]))
    mine, other = record[0], swapped(record[1])
    squared, *held = lax.optimization_barrier((squared, *held))
    partner = swapped(squared)

    chunks = 4
    held = [pltpu.with_memory_space_constraint(array, pltpu.VMEM) for array in held]
    new_query, new_keyval, new_output, losses, new_gains, layer_outputs = pl.pallas_call(
        functools.partial(update_kernel, float(tokens * full), chunks),
        in_specs=[SMEM] + [VMEM] * 12,
        out_specs=[far] * 3 + [SMEM] + [VMEM] * 2,
        out_shape=[pltpu.HBM(w.shape, jnp.bfloat16) for w in arrays[:3]]
        + [
            jax.ShapeDtypeStruct((1, 2), jnp.float32),
            jax.ShapeDtypeStruct((1, full), jnp.float32),
            jax.ShapeDtypeStruct((1, 2) + mine.shape, jnp.bfloat16),
        ],
        scratch_shapes=[pltpu.VMEM(w.shape, jnp.bfloat16) for w in arrays[:3]]
        + [pltpu.SemaphoreType.DMA((3, chunks))],
        compiler_params=limit(14),
    )(
        core.reshape(1), squared, partner, norm_gains, gain_noise[None], mine, other,
        *held,
    )
    return (
        layer_outputs,
        losses,
        new_gains,
        new_query[None, None],
        new_keyval[None, None],
        new_output[None, None],
    )


def solution(mesh):
    mesh = Mesh(mesh.devices.reshape(-1, NY, NZ, NC), ("section", "y", "z", "core"))
    tensor = ("y", "z", "core")
    return jax.shard_map(
        local,
        mesh=mesh,
        in_specs=(
            P(None, tensor),
            P(None, tensor),
            P("section", None),
            P("section", tensor, None, None),
            P("section", tensor, None, None),
            P("section", tensor, None, None),
            P(),
            P(),
        ),
        out_specs=(
            P("section", None, None, tensor),
            P("section", None),
            P("section", None),
            P("section", tensor, None, None),
            P("section", tensor, None, None),
            P("section", tensor, None, None),
        ),
        check_vma=False,
    )
```
